128 devices in a mesh: grp: 2 (over core), dev: 64 (over y, z, x).
Axes of the slice: x: 4, y: 4, z: 4, core: 2. Of those that a mesh axis runs over, the one named last changes fastest.
Arguments:
- hidden_state: bfloat16 [3, 256, 7168], P(None, ('grp', 'dev')), may hold values from -180 to 180
- ffn_gain: bfloat16 [7168], replicated, may hold values from 0.5 to 1.5
- expert_ids: int32 [3, 256, 8], P(None, ('grp', 'dev')), may hold values from 0 to 15, all different within a row; in each aligned block of 256 rows (0 to 255, 256 to 511, ..., all dimensions but the last counted through in order) at most 192 rows name the same one
- expert_gates: bfloat16 [3, 256, 8], P(None, ('grp', 'dev')), may hold values from 0.049804688 to 0.796875
- w_gate: bfloat16 [7168, 32768], P(None, ('grp', 'dev')), may hold values from -0.0625 to 0.0625
- w_up: bfloat16 [7168, 32768], P(None, ('grp', 'dev')), may hold values from -0.0625 to 0.0625
- w_down: bfloat16 [32768, 7168], P(('grp', 'dev')), may hold values from -0.125 to 0.125
- queries: bfloat16 [3, 256, 128, 576], P(None, ('grp', 'dev')), may hold values from -36 to 36
- kv_cache: bfloat16 [256, 2048, 576], P(('grp', 'dev')), may hold values from -6 to 6
- new_keys: bfloat16 [3, 256, 576], P(None, ('grp', 'dev')), may hold values from -6 to 6
- cache_lengths: int32 [256], P(('grp', 'dev')), may hold values from 256 to 2048, as said below
Outputs:
- attended: bfloat16 [3, 256, 128, 512], P(None, ('grp', 'dev'))
- routed: bfloat16 [3, 256, 7168], P(None, ('grp', 'dev'))
The draws below stay inside these ranges and needn't reach their ends.
Inputs may be any that keep to these rules, and one draw needn't show every extreme that they name: `expert_ids`: in each step no expert is picked by more than 192 of the 256 tokens; some expert is picked by exactly 192 tokens in some step. `cache_lengths`: some request has all 2048 slots filled.
All inputs are finite; a program needn't handle non-finite values.
Results may differ from the reference program's by a relative error of at most 0.0065.
Values may be sent and summed in bfloat16 or wider, within the bound.
No kernel may reach another device: no remote copies, remote signals or barrier semaphores. Data moves between devices by JAX's collectives and lax.ppermute only.
A program may use at most 192 MiB of HBM per device.

```python
import math
import jax
import jax.numpy as jnp
import numpy as np
from jax import lax

D = 7168
FFE = 2048
HEADS = 128
KV_RANK = 512
TOP = 8
EXPERTS = 16
STEPS = 3
CACHE = 2048
LAT = 576
REQUESTS = 256
CAP = 192


def fresh_values(key):
    return jnp.clip(jax.random.normal(key, (STEPS, REQUESTS, LAT), jnp.float32), -6.0, 6.0)


def draw_new_keys(key, part):
    values = fresh_values(key)
    return values.astype(jnp.bfloat16)


def draw_queries(key, part):
    fresh = fresh_values(key)
    key = jax.random.fold_in(key, 11)
    full_shape = (STEPS, REQUESTS, HEADS, LAT)
    noise_part = jnp.clip(jax.random.normal(key, full_shape, jnp.float32), -6.0, 6.0)
    values = noise_part + 0.2 * fresh[:, :, None, :]
    return values.astype(jnp.bfloat16)


def draw_kv_cache(key, part):
    key = jax.random.fold_in(key, 23)
    full_shape = (REQUESTS, CACHE, LAT)
    values = jnp.clip(jax.random.normal(key, full_shape, jnp.float32), -6.0, 6.0)
    return values.astype(jnp.bfloat16)


def draw_cache_lengths(key, part):
    key = jax.random.fold_in(key, 37)
    first_key, second_key = jax.random.split(key)
    values = jax.random.randint(first_key, (REQUESTS,), CACHE // 8, CACHE + 1)
    fullest = jax.random.randint(second_key, (), 0, REQUESTS)
    return jnp.where(jnp.arange(REQUESTS) == fullest, CACHE, values).astype(jnp.int32)


def draw_hidden_state(key, part):
    key = jax.random.fold_in(key, 5)
    split_keys = jax.random.split(key, 3)
    full_shape = (STEPS, REQUESTS, D)
    row_scale = jnp.exp(jax.random.uniform(split_keys[0], (STEPS, REQUESTS, 1), jnp.float32, 0.0, math.log(10.0)))
    col_scale = jnp.exp(jax.random.uniform(split_keys[1], (D,), jnp.float32, math.log(0.3), math.log(3.0)))
    base_values = jnp.clip(jax.random.normal(split_keys[2], full_shape, jnp.float32), -6.0, 6.0)
    return (base_values * row_scale * col_scale).astype(jnp.bfloat16)


def shard_levels(key, extent, shards, low, top_value):
    def one(position, parts):
        steps = jax.random.uniform(jax.random.fold_in(jax.random.fold_in(key, 6), position), (parts,), jnp.float32, low / len(shards), top_value / len(shards))
        return jnp.repeat(jnp.exp(steps), extent[position] // parts).reshape((-1,) + (1,) * (len(extent) - position - 1))

    loudness = one(*shards[0])
    for cut in shards[1:]:
        loudness = loudness * one(*cut)
    return loudness


def shared_out(key, own, number, rows, number_of, top, most, skew):
    order = jax.random.permutation(key, number_of)
    heavy_load, usual = shares(number_of, rows * top, most, skew, True), shares(number_of, rows * top, most, skew, False)
    places = jnp.arange(number_of)

    def named(sizes, rotation):
        used = int((sizes > 0).sum())
        fixed = max(1, used // 4)
        moved = fixed + (places - fixed + rotation * (used - fixed)) % max(1, number_of - fixed)
        return jnp.zeros((number_of,), jnp.int32).at[order[jnp.where(places < fixed, places, moved)]].set(jnp.asarray(sizes, jnp.int32))

    sizes = jnp.where(number % 4 == 0, named(heavy_load, number // 4), named(usual, number - number // 4 - 1))
    mixed = jax.random.permutation(jax.random.fold_in(own, 3), number_of)
    donor, sink = mixed[0:number_of // 2 * 2:2], mixed[1:number_of // 2 * 2:2]
    margin = jnp.minimum(sizes[donor] - 1, most - sizes[sink]) // 2
    margin = jnp.where((donor == order[0]) | (sink == order[0]) | (sizes[sink] == 0), 0, jnp.maximum(margin, 0))
    moved = jax.random.randint(jax.random.fold_in(own, 4), (number_of // 2,), 0, 1 << 20) % (margin + 1)
    sizes = sizes.at[donor].add(-moved).at[sink].add(moved)
    members = jnp.searchsorted(jnp.cumsum(sizes), jnp.arange(rows * top), side="right").astype(jnp.int32)
    grid = members.reshape(top, rows).T
    grid = grid[jax.random.permutation(jax.random.fold_in(own, 1), rows)]
    rotation = jax.random.randint(jax.random.fold_in(own, 2), (rows, 1), 0, top)
    return jnp.take_along_axis(grid, (jnp.arange(top)[None, :] + rotation) % top, axis=1)


def shares(count, total, limit, lean, full):
    portions = [(1 << 20) // math.isqrt(grade ** lean) + 1 for grade in range(1, count + 1)]
    largest = limit if full else min(limit, max(-(-total // count), total * portions[0] // sum(portions)))
    least = 1 if total - largest >= count - 1 else 0
    counts, surplus = [largest] + [least] * (count - 1), total - largest - least * (count - 1)
    while surplus > 0:
        free = [i for i in range(1, count) if counts[i] < largest] or [i for i in range(1, count) if counts[i] < limit]
        pool, remaining = sum([portions[i] for i in free]), surplus
        for i in free:
            more = min(limit - counts[i], max(1, remaining * portions[i] // pool), surplus)
            counts[i] = counts[i] + more
            surplus = surplus - more
    return np.array(counts)


def scatter_about(stream_key, dims, deviation, most, cuts=(), held_as=jnp.bfloat16):
    level = shard_levels(stream_key, dims, cuts, -0.22, 0.18) if cuts else 1.0
    drawn = jax.random.normal(stream_key, dims, jnp.float32) * deviation * level
    return jnp.minimum(jnp.maximum(drawn, -most), most).astype(held_as)


def setup_inputs(seed: int = 0) -> dict:
    arg_keys = jax.random.split(jax.random.key(seed), 12)
    hidden_state = draw_hidden_state(jax.random.fold_in(arg_keys[11], 71), 0)
    ffn_gain = jnp.clip(1.0 + 0.1 * jax.random.normal(arg_keys[1], (D,), jnp.float32), 0.5, 1.5).astype(jnp.bfloat16)
    expert_ids_keys = jax.random.split(jax.random.fold_in(arg_keys[2], 1), STEPS * REQUESTS // REQUESTS)
    expert_ids_turns = jax.random.permutation(jax.random.fold_in(arg_keys[2], 3), STEPS * REQUESTS // REQUESTS)
    expert_ids = jax.vmap(lambda own, number: shared_out(jax.random.fold_in(arg_keys[2], 2), own, number, REQUESTS, EXPERTS, TOP, CAP, 2))(expert_ids_keys, expert_ids_turns).reshape((STEPS, REQUESTS, TOP))
    expert_gates = jnp.clip(jnp.exp(math.log(0.796875) - 2.7725887 * jax.random.uniform(arg_keys[3], (STEPS, REQUESTS, TOP), jnp.float32) ** shard_levels(arg_keys[3], (STEPS, REQUESTS, TOP), ((1, 128),), -0.2, 0.2)), 0.049804688, 0.796875).astype(jnp.bfloat16)
    w_gate = scatter_about(arg_keys[4], (D, EXPERTS * FFE), D ** -0.5, 0.0625, ((1, 128),))
    w_up = scatter_about(arg_keys[5], (D, EXPERTS * FFE), D ** -0.5, 0.0625, ((1, 128),))
    w_down = scatter_about(arg_keys[6], (EXPERTS * FFE, D), FFE ** -0.5, 0.125, ((0, 128),))
    queries = draw_queries(jax.random.fold_in(arg_keys[11], 71), 0)
    kv_cache = draw_kv_cache(jax.random.fold_in(arg_keys[11], 71), 0)
    new_keys = draw_new_keys(jax.random.fold_in(arg_keys[11], 71), 0)
    cache_lengths = draw_cache_lengths(jax.random.fold_in(arg_keys[11], 71), 0)
    return dict(hidden_state=hidden_state, ffn_gain=ffn_gain, expert_ids=expert_ids, expert_gates=expert_gates, w_gate=w_gate, w_up=w_up, w_down=w_down, queries=queries, kv_cache=kv_cache, new_keys=new_keys, cache_lengths=cache_lengths)


EPS = 1e-06
SCORE_SCALE = 1.0 / math.sqrt(192.0)

def normalize(state_rows, gain_row):
    values = state_rows.astype(jnp.float32)
    factor = lax.rsqrt(lax.optimization_barrier(jnp.mean(values * values, axis=-1, keepdims=True)) + EPS)
    return (values * factor * gain_row.astype(jnp.float32)).astype(jnp.bfloat16)

def dense_gates(id_rows, gate_rows, expert_count):
    lanes = jnp.arange(expert_count, dtype=jnp.int32)
    matches = id_rows[:, :, None] == lanes[None, None, :]
    spread = jnp.where(matches, gate_rows[:, :, None].astype(jnp.float32), 0.0)
    return lax.optimization_barrier(jnp.sum(spread, axis=1)).astype(jnp.bfloat16)

def reference(hidden_state, ffn_gain, expert_ids, expert_gates, w_gate, w_up, w_down, queries, kv_cache, new_keys, cache_lengths):

    def moe_step(unused_carry, inputs):
        state_rows, id_rows, gate_rows = inputs
        normed = normalize(state_rows, ffn_gain)
        gate_table = dense_gates(id_rows, gate_rows, EXPERTS).astype(jnp.float32)

        def add_expert(expert, running):
            start_col = (expert * FFE).astype(jnp.int32)
            gate_cols = lax.dynamic_slice_in_dim(w_gate, start_col, FFE, 1)
            up_cols = lax.dynamic_slice_in_dim(w_up, start_col, FFE, 1)
            down_rows = lax.dynamic_slice_in_dim(w_down, start_col, FFE, 0)
            gate_proj = jnp.dot(normed, gate_cols, preferred_element_type=jnp.float32)
            up_proj = jnp.dot(normed, up_cols, preferred_element_type=jnp.float32)
            hidden = (jax.nn.silu(gate_proj) * up_proj).astype(jnp.bfloat16)
            expert_out = jnp.dot(hidden, down_rows, preferred_element_type=jnp.float32)
            lane_mask = jnp.arange(EXPERTS, dtype=jnp.int32) == expert.astype(jnp.int32)
            column = lax.optimization_barrier(jnp.sum(jnp.where(lane_mask[None, :], gate_table, 0.0), axis=1))
            return running + expert_out * column[:, None]
        running = lax.fori_loop(0, EXPERTS, add_expert, jnp.zeros((REQUESTS, D), jnp.float32))
        return (unused_carry, running.astype(jnp.bfloat16))
    unused_carry, routed = lax.scan(moe_step, jnp.zeros((), jnp.float32), (hidden_state, expert_ids, expert_gates))
    flat_queries = queries.reshape(STEPS * REQUESTS, HEADS, LAT)
    request_ids = jnp.tile(jnp.arange(REQUESTS, dtype=jnp.int32), STEPS)
    step_ids = jnp.repeat(jnp.arange(STEPS, dtype=jnp.int32), REQUESTS)

    def attend_one(inputs):
        query_rows, request_id, step_id = inputs
        cache_rows = lax.dynamic_index_in_dim(kv_cache, request_id, 0, keepdims=False)
        fresh_rows = lax.dynamic_index_in_dim(new_keys, request_id, 1, keepdims=False)
        length = lax.dynamic_index_in_dim(cache_lengths, request_id, 0, keepdims=False)
        key_rows = jnp.concatenate([cache_rows, fresh_rows], axis=0)
        valid_mask = jnp.concatenate([jnp.arange(CACHE, dtype=jnp.int32) < length, jnp.arange(STEPS, dtype=jnp.int32) <= step_id])
        scores = jnp.dot(query_rows, key_rows.T, preferred_element_type=jnp.float32) * SCORE_SCALE
        scores = jnp.where(valid_mask[None, :], scores, -jnp.inf)
        weights_bf = jax.nn.softmax(scores, axis=-1).astype(jnp.bfloat16)
        return jnp.dot(weights_bf, key_rows[:, :KV_RANK], preferred_element_type=jnp.float32).astype(jnp.bfloat16)
    attended = lax.map(attend_one, (flat_queries, request_ids, step_ids))
    attended = attended.reshape(STEPS, REQUESTS, HEADS, KV_RANK)
    return (attended, routed)
```

```python
import math

import jax
import jax.numpy as jnp
from jax import lax
from jax.experimental import pallas as pl
from jax.experimental.pallas import tpu as pltpu
from jax.sharding import Mesh
from jax.sharding import PartitionSpec as P

KV_RANK = 512
EXPERTS = 16
EPS = 1e-06
SCORE_SCALE = 1.0 / math.sqrt(192.0)
AXES = ("c", "y", "z", "x")
SIDE = 4
GATE_LANES = 128
SLOT_CHUNK = 512
FEATURE_CHUNK = 1792
VMEM_LIMIT = 48 * 1024 * 1024


def device_number(c, y, z, x):
    return ((c * SIDE + y) * SIDE + z) * SIDE + x


def shifted_pairs(axis_of_core, distance):
    pairs = []
    for c in range(2):
        for y in range(SIDE):
            for z in range(SIDE):
                for x in range(SIDE):
                    place = {"y": y, "z": z, "x": x}
                    axis = axis_of_core[c]
                    place[axis] = (place[axis] + distance) % SIDE
                    pairs.append((device_number(c, y, z, x), device_number(c, **place)))
    return pairs


def shift(block, axis_of_core, distance):
    return lax.ppermute(block, AXES, shifted_pairs(axis_of_core, distance))


def other_core(block):
    return lax.ppermute(block, "c", [(0, 1), (1, 0)])


def collect(block, axis_of_core):
    return [
        block,
        shift(block, axis_of_core, -1),
        shift(block, axis_of_core, 1),
        shift(block, axis_of_core, 2),
    ]


def hand_back(blocks, axis_of_core):
    received = [
        blocks[0],
        shift(blocks[1], axis_of_core, 1),
        shift(blocks[2], axis_of_core, -1),
        shift(blocks[3], axis_of_core, 2),
    ]
    total = received[0].astype(jnp.float32)
    for block in received[1:]:
        total = total + block.astype(jnp.float32)
    return total.astype(jnp.bfloat16)


def cut(rows, parts):
    size = rows.shape[0] // parts
    return [rows[i * size : (i + 1) * size] for i in range(parts)]


def normalize(state_rows, gain_row):
    values = state_rows.astype(jnp.float32)
    factor = lax.rsqrt(jnp.mean(values * values, axis=-1, keepdims=True) + EPS)
    return (values * factor * gain_row.astype(jnp.float32)).astype(jnp.bfloat16)


def dense_gates(id_rows, gate_rows, lane_count):
    lanes = jnp.arange(lane_count, dtype=jnp.int32)
    matches = id_rows[:, :, None] == lanes[None, None, :]
    spread = jnp.where(matches, gate_rows[:, :, None].astype(jnp.float32), 0.0)
    return jnp.sum(spread, axis=1).astype(jnp.bfloat16)


def attend_body(length_ref, q_ref, k_ref, fresh_ref, out_ref, score_ref):
    request = pl.program_id(0)
    length = length_ref[request]
    steps, heads = q_ref.shape[0], q_ref.shape[3]
    slots = k_ref.shape[2]
    q = jnp.concatenate([q_ref[s, 0].T for s in range(steps)], axis=0)
    fresh = fresh_ref[0]
    fresh_scores = (
        lax.dot_general(q, fresh, (((1,), (1,)), ((), ())), preferred_element_type=jnp.float32)
        * SCORE_SCALE
    )
    row_step = lax.broadcasted_iota(jnp.int32, fresh_scores.shape, 0) // heads
    fresh_lane = lax.broadcasted_iota(jnp.int32, fresh_scores.shape, 1)
    fresh_scores = jnp.where(fresh_lane <= row_step, fresh_scores, -jnp.inf)
    top = jnp.max(fresh_scores, axis=1, keepdims=True)
    for start in range(0, slots, SLOT_CHUNK):
        cols = pl.ds(start, SLOT_CHUNK)
        scores = jnp.dot(q, k_ref[0, :, cols], preferred_element_type=jnp.float32) * SCORE_SCALE
        slot = lax.broadcasted_iota(jnp.int32, scores.shape, 1) + start
        scores = jnp.where(slot < length, scores, -jnp.inf)
        score_ref[:, cols] = scores
        top = jnp.maximum(top, jnp.max(scores, axis=1, keepdims=True))
    fresh_exp = jnp.exp(fresh_scores - top)
    denominator = jnp.sum(fresh_exp, axis=1, keepdims=True)
    total = jnp.dot(
        fresh_exp.astype(jnp.bfloat16), fresh[:, :KV_RANK], preferred_element_type=jnp.float32
    )
    for start in range(0, slots, SLOT_CHUNK):
        cols = pl.ds(start, SLOT_CHUNK)
        weights = jnp.exp(score_ref[:, cols] - top)
        denominator = denominator + jnp.sum(weights, axis=1, keepdims=True)
        total = total + lax.dot_general(
            weights.astype(jnp.bfloat16),
            k_ref[0, :KV_RANK, cols],
            (((1,), (1,)), ((), ())),
            preferred_element_type=jnp.float32,
        )
    result = (total / denominator).astype(jnp.bfloat16)
    for s in range(steps):
        out_ref[s, 0] = result[s * heads : (s + 1) * heads]


def attend(queries, kv_cache, new_keys, cache_lengths):
    steps, requests, heads, width = queries.shape
    slots = kv_cache.shape[1]
    q_t = jnp.swapaxes(queries, 2, 3)
    k_t = jnp.swapaxes(kv_cache, 1, 2)
    fresh = jnp.pad(jnp.swapaxes(new_keys, 0, 1), ((0, 0), (0, 16 - steps), (0, 0)))
    return pl.pallas_call(
        attend_body,
        out_shape=jax.ShapeDtypeStruct((steps, requests, heads, KV_RANK), jnp.bfloat16),
        grid=(requests,),
        in_specs=[
            pl.BlockSpec(memory_space=pltpu.SMEM),
            pl.BlockSpec((steps, 1, width, heads), lambda r: (0, r, 0, 0)),
            pl.BlockSpec((1, width, slots), lambda r: (r, 0, 0)),
            pl.BlockSpec((1, 16, width), lambda r: (r, 0, 0)),
        ],
        out_specs=pl.BlockSpec((steps, 1, heads, KV_RANK), lambda r: (0, r, 0, 0)),
        scratch_shapes=[pltpu.VMEM((steps * heads, slots), jnp.float32)],
        compiler_params=pltpu.CompilerParams(vmem_limit_bytes=VMEM_LIMIT),
        cost_estimate=pl.CostEstimate(
            flops=2 * steps * requests * heads * slots * (width + KV_RANK),
            bytes_accessed=2 * requests * (slots * width + steps * heads * (width + KV_RANK)),
            transcendentals=steps * requests * heads * slots,
        ),
        name="attend",
    )(cache_lengths, q_t, k_t, fresh)


def expert_call(blocks, my_lane, w_gate, w_up, w_down):
    count = len(blocks)
    rows = blocks[0].shape[0]
    features = w_gate.shape[0]
    hidden_units = w_gate.shape[1]
    chunks = features // FEATURE_CHUNK
    last = chunks - 1
    all_rows = rows * count

    def body(*refs):
        token_refs, gate_refs = refs[:count], refs[count : 2 * count]
        lane_ref, gate_w, up_w, down_w = refs[2 * count : 2 * count + 4]
        out_refs = refs[2 * count + 4 : 3 * count + 4]
        gate_acc, up_acc, hidden_ref, column_ref = refs[3 * count + 4 :]
        at = pl.program_id(0)

        @pl.when(at == 0)
        def _():
            gate_acc[...] = jnp.zeros_like(gate_acc)
            up_acc[...] = jnp.zeros_like(up_acc)
            gates = jnp.concatenate([r[...].astype(jnp.float32) for r in gate_refs], axis=0)
            column_ref[...] = jnp.sum(gates * lane_ref[...], axis=1, keepdims=True)

        @pl.when(at < chunks)
        def _():
            tokens = jnp.concatenate([r[...] for r in token_refs], axis=0)
            gate_acc[...] += jnp.dot(tokens, gate_w[...], preferred_element_type=jnp.float32)
            up_acc[...] += jnp.dot(tokens, up_w[...], preferred_element_type=jnp.float32)

        @pl.when(at == last)
        def _():
            gate = gate_acc[...]
            hidden_ref[...] = (gate / (1.0 + jnp.exp(-gate)) * up_acc[...]).astype(jnp.bfloat16)

        @pl.when(at >= chunks)
        def _():
            outs = jnp.dot(hidden_ref[...], down_w[...], preferred_element_type=jnp.float32)
            outs = (outs * column_ref[...]).astype(jnp.bfloat16)
            for i, out_ref in enumerate(out_refs):
                out_ref[...] = outs[i * rows : (i + 1) * rows]

    def inward(i):
        return jnp.minimum(i, last)

    def outward(i):
        return jnp.maximum(i - chunks, 0)

    return pl.pallas_call(
        body,
        out_shape=[jax.ShapeDtypeStruct((rows, features), jnp.bfloat16)] * count,
        grid=(2 * chunks,),
        in_specs=[pl.BlockSpec((rows, FEATURE_CHUNK), lambda i: (0, inward(i)))] * count
        + [pl.BlockSpec((rows, GATE_LANES), lambda i: (0, features // GATE_LANES))] * count
        + [
            pl.BlockSpec((1, GATE_LANES), lambda i: (0, 0)),
            pl.BlockSpec((FEATURE_CHUNK, hidden_units), lambda i: (inward(i), 0)),
            pl.BlockSpec((FEATURE_CHUNK, hidden_units), lambda i: (inward(i), 0)),
            pl.BlockSpec((hidden_units, FEATURE_CHUNK), lambda i: (0, outward(i))),
        ],
        out_specs=[pl.BlockSpec((rows, FEATURE_CHUNK), lambda i: (0, outward(i)))] * count,
        scratch_shapes=[
            pltpu.VMEM((all_rows, hidden_units), jnp.float32),
            pltpu.VMEM((all_rows, hidden_units), jnp.float32),
            pltpu.VMEM((all_rows, hidden_units), jnp.bfloat16),
            pltpu.VMEM((all_rows, 1), jnp.float32),
        ],
        compiler_params=pltpu.CompilerParams(vmem_limit_bytes=VMEM_LIMIT),
        cost_estimate=pl.CostEstimate(
            flops=6 * all_rows * features * hidden_units,
            bytes_accessed=2 * (3 * features * hidden_units + 2 * all_rows * features),
            transcendentals=all_rows * hidden_units,
        ),
        name="experts",
    )(*blocks, *blocks, my_lane, w_gate, w_up, w_down)


def routed_block(hidden_state, ffn_gain, expert_ids, expert_gates, w_gate, w_up, w_down):
    steps, requests, features = hidden_state.shape
    tokens = steps * requests
    normed = normalize(hidden_state.reshape(tokens, features), ffn_gain)
    gates = dense_gates(
        expert_ids.reshape(tokens, -1), expert_gates.reshape(tokens, -1), GATE_LANES
    )
    own = jnp.concatenate([normed, gates], axis=1)
    near, middle, far = ("z", "z"), ("y", "x"), ("x", "y")
    own = jnp.concatenate(collect(own, near), axis=0)
    own = jnp.concatenate(collect(own, middle), axis=0)
    quarters = collect(own, far)
    others = [other_core(q) for q in quarters]
    groups = lax.axis_size(AXES)
    my_expert = lax.axis_index(AXES) // (groups // EXPERTS)
    my_lane = (jnp.arange(GATE_LANES, dtype=jnp.int32) == my_expert).astype(jnp.float32)[None, :]
    mine, theirs = [None] * SIDE, [None] * SIDE
    for members in ((0,), (1, 2), (3,)):
        blocks = [quarters[i] for i in members] + [others[i] for i in members]
        outs = expert_call(blocks, my_lane, w_gate, w_up, w_down)
        for j, i in enumerate(members):
            mine[i] = outs[j]
            theirs[i] = outs[len(members) + j]
    sums = [
        (a.astype(jnp.float32) + other_core(b).astype(jnp.float32)).astype(jnp.bfloat16)
        for a, b in zip(mine, theirs)
    ]
    summed = hand_back(sums, far)
    summed = hand_back(cut(summed, SIDE), middle)
    summed = hand_back(cut(summed, SIDE), near)
    return summed.reshape(steps, requests, features)


def on_device(
    hidden_state,
    ffn_gain,
    expert_ids,
    expert_gates,
    w_gate,
    w_up,
    w_down,
    queries,
    kv_cache,
    new_keys,
    cache_lengths,
):
    routed = routed_block(
        hidden_state, ffn_gain, expert_ids, expert_gates, w_gate, w_up, w_down
    )
    attended = attend(queries, kv_cache, new_keys, cache_lengths)
    return attended, routed


def solution(mesh):
    chips = Mesh(mesh.devices.reshape(2, SIDE, SIDE, SIDE), AXES)
    placed = (
        P(None, AXES, None),
        P(),
        P(None, AXES, None),
        P(None, AXES, None),
        P(None, AXES),
        P(None, AXES),
        P(AXES, None),
        P(None, AXES, None, None),
        P(AXES, None, None),
        P(None, AXES, None),
        P(AXES),
    )
    return jax.shard_map(
        on_device,
        mesh=chips,
        in_specs=placed,
        out_specs=(P(None, AXES, None, None), P(None, AXES, None)),
        check_vma=False,
    )
```

```python
import math

import jax
import jax.numpy as jnp
from jax import lax
from jax.experimental import pallas as pl
from jax.experimental.pallas import tpu as pltpu
from jax.sharding import Mesh
from jax.sharding import PartitionSpec as P

KV_RANK = 512
EXPERTS = 16
EPS = 1e-06
SCORE_SCALE = 1.0 / math.sqrt(192.0)
AXES = ("c", "y", "z", "x")
SIDE = 4
GATE_LANES = 128
SLOT_CHUNK = 512
FEATURE_CHUNK = 3584
ATTEND_VMEM = 20 * 1024 * 1024
EXPERT_VMEM = 32 * 1024 * 1024


def device_number(c, y, z, x):
    return ((c * SIDE + y) * SIDE + z) * SIDE + x


def shifted_pairs(axis_of_core, distance):
    pairs = []
    for c in range(2):
        for y in range(SIDE):
            for z in range(SIDE):
                for x in range(SIDE):
                    place = {"y": y, "z": z, "x": x}
                    axis = axis_of_core[c]
                    place[axis] = (place[axis] + distance) % SIDE
                    pairs.append((device_number(c, y, z, x), device_number(c, **place)))
    return pairs


def shift(block, axis_of_core, distance):
    return lax.ppermute(block, AXES, shifted_pairs(axis_of_core, distance))


def other_core(block):
    return lax.ppermute(block, "c", [(0, 1), (1, 0)])


def collect(block, axis_of_core):
    return [
        block,
        shift(block, axis_of_core, -1),
        shift(block, axis_of_core, 1),
        shift(block, axis_of_core, 2),
    ]


def send_home(blocks, axis_of_core):
    return [
        blocks[0],
        shift(blocks[1], axis_of_core, 1),
        shift(blocks[2], axis_of_core, -1),
        shift(blocks[3], axis_of_core, 2),
    ]


def add_up(blocks):
    total = blocks[0].astype(jnp.float32)
    for block in blocks[1:]:
        total = total + block.astype(jnp.float32)
    return total.astype(jnp.bfloat16)


def cut(rows, parts):
    size = rows.shape[0] // parts
    return [rows[i * size : (i + 1) * size] for i in range(parts)]


def prepare_body(state_ref, gain_ref, id_ref, gate_ref, out_ref):
    steps, requests, features = state_ref.shape
    gain = gain_ref[...].astype(jnp.float32)
    for s in range(steps):
        rows = pl.ds(s * requests, requests)
        values = state_ref[s].astype(jnp.float32)
        factor = lax.rsqrt(jnp.mean(values * values, axis=-1, keepdims=True) + EPS)
        out_ref[rows, :features] = (values * factor * gain).astype(jnp.bfloat16)
        ids, gates = id_ref[s], gate_ref[s].astype(jnp.float32)
        lanes = lax.broadcasted_iota(jnp.int32, (requests, GATE_LANES), 1)
        table = jnp.zeros((requests, GATE_LANES), jnp.float32)
        for k in range(ids.shape[1]):
            table = table + jnp.where(lanes == ids[:, k : k + 1], gates[:, k : k + 1], 0.0)
        out_ref[rows, features:] = table.astype(jnp.bfloat16)


def prepare(hidden_state, ffn_gain, expert_ids, expert_gates):
    steps, requests, features = hidden_state.shape
    return pl.pallas_call(
        prepare_body,
        out_shape=jax.ShapeDtypeStruct((steps * requests, features + GATE_LANES), jnp.bfloat16),
        name="prepare",
    )(hidden_state, ffn_gain[None, :], expert_ids, expert_gates)


def stack_body(*refs):
    rows = refs[0].shape[0]
    for i, ref in enumerate(refs[:-1]):
        refs[-1][pl.ds(i * rows, rows), :] = ref[...]


def stack(blocks):
    rows, width = blocks[0].shape
    return pl.pallas_call(
        stack_body,
        out_shape=jax.ShapeDtypeStruct((rows * len(blocks), width), blocks[0].dtype),
        name="stack",
    )(*blocks)


def attend_body(length_ref, q_ref, k_ref, fresh_ref, out_ref, score_ref):
    request = pl.program_id(0)
    length = length_ref[request]
    steps, heads = q_ref.shape[0], q_ref.shape[3]
    slots = k_ref.shape[2]
    q = jnp.concatenate([q_ref[s, 0].T for s in range(steps)], axis=0)
    fresh = fresh_ref[0]
    fresh_scores = (
        lax.dot_general(q, fresh, (((1,), (1,)), ((), ())), preferred_element_type=jnp.float32)
        * SCORE_SCALE
    )
    row_step = lax.broadcasted_iota(jnp.int32, fresh_scores.shape, 0) // heads
    fresh_lane = lax.broadcasted_iota(jnp.int32, fresh_scores.shape, 1)
    fresh_scores = jnp.where(fresh_lane <= row_step, fresh_scores, -jnp.inf)
    top = jnp.max(fresh_scores, axis=1, keepdims=True)
    for start in range(0, slots, SLOT_CHUNK):
        cols = pl.ds(start, SLOT_CHUNK)
        scores = jnp.dot(q, k_ref[0, :, cols], preferred_element_type=jnp.float32) * SCORE_SCALE
        slot = lax.broadcasted_iota(jnp.int32, scores.shape, 1) + start
        scores = jnp.where(slot < length, scores, -jnp.inf)
        score_ref[:, cols] = scores
        top = jnp.maximum(top, jnp.max(scores, axis=1, keepdims=True))
    fresh_exp = jnp.exp(fresh_scores - top)
    denominator = jnp.sum(fresh_exp, axis=1, keepdims=True)
    total = jnp.dot(
        fresh_exp.astype(jnp.bfloat16), fresh[:, :KV_RANK], preferred_element_type=jnp.float32
    )
    for start in range(0, slots, SLOT_CHUNK):
        cols = pl.ds(start, SLOT_CHUNK)
        weights = jnp.exp(score_ref[:, cols] - top)
        denominator = denominator + jnp.sum(weights, axis=1, keepdims=True)
        total = total + lax.dot_general(
            weights.astype(jnp.bfloat16),
            k_ref[0, :KV_RANK, cols],
            (((1,), (1,)), ((), ())),
            preferred_element_type=jnp.float32,
        )
    result = (total / denominator).astype(jnp.bfloat16)
    for s in range(steps):
        out_ref[s, 0] = result[s * heads : (s + 1) * heads]


def attend(queries, kv_cache, new_keys, cache_lengths):
    steps, requests, heads, width = queries.shape
    slots = kv_cache.shape[1]
    q_t = jnp.swapaxes(queries, 2, 3)
    k_t = jnp.swapaxes(kv_cache, 1, 2)
    fresh = jnp.pad(jnp.swapaxes(new_keys, 0, 1), ((0, 0), (0, 16 - steps), (0, 0)))
    return pl.pallas_call(
        attend_body,
        out_shape=jax.ShapeDtypeStruct((steps, requests, heads, KV_RANK), jnp.bfloat16),
        grid=(requests,),
        in_specs=[
            pl.BlockSpec(memory_space=pltpu.SMEM),
            pl.BlockSpec((steps, 1, width, heads), lambda r: (0, r, 0, 0)),
            pl.BlockSpec((1, width, slots), lambda r: (r, 0, 0)),
            pl.BlockSpec((1, 16, width), lambda r: (r, 0, 0)),
        ],
        out_specs=pl.BlockSpec((steps, 1, heads, KV_RANK), lambda r: (0, r, 0, 0)),
        scratch_shapes=[pltpu.VMEM((steps * heads, slots), jnp.float32)],
        compiler_params=pltpu.CompilerParams(vmem_limit_bytes=ATTEND_VMEM),
        cost_estimate=pl.CostEstimate(
            flops=2 * steps * requests * heads * slots * (width + KV_RANK),
            bytes_accessed=2 * requests * (slots * width + steps * heads * (width + KV_RANK)),
            transcendentals=steps * requests * heads * slots,
        ),
        name="attend",
    )(cache_lengths, q_t, k_t, fresh)


def hold_body(*refs):
    pass


def hold(blocks, after):
    anywhere = pl.BlockSpec(memory_space=pl.ANY)
    return pl.pallas_call(
        hold_body,
        out_shape=[jax.ShapeDtypeStruct(b.shape, b.dtype) for b in blocks],
        in_specs=[anywhere] * (len(blocks) + len(after)),
        out_specs=[anywhere] * len(blocks),
        input_output_aliases={i: i for i in range(len(blocks))},
        compiler_params=pltpu.CompilerParams(vmem_limit_bytes=1024 * 1024),
        name="hold",
    )(*blocks, *after)


def expert_call(blocks, my_lane, w_gate, w_up, w_down, after):
    count = len(blocks)
    rows = blocks[0].shape[0]
    features = w_gate.shape[0]
    hidden_units = w_gate.shape[1]
    chunks = features // FEATURE_CHUNK
    last = chunks - 1
    all_rows = rows * count
    first_out = 2 * count + 4 + len(after)

    def body(*refs):
        token_refs, gate_refs = refs[:count], refs[count : 2 * count]
        lane_ref, gate_w, up_w, down_w = refs[2 * count : 2 * count + 4]
        out_refs = refs[first_out : first_out + count]
        gate_acc, up_acc, hidden_ref, column_ref = refs[first_out + count :]
        at = pl.program_id(0)

        @pl.when(at == 0)
        def _():
            gate_acc[...] = jnp.zeros_like(gate_acc)
            up_acc[...] = jnp.zeros_like(up_acc)
            gates = jnp.concatenate([r[...].astype(jnp.float32) for r in gate_refs], axis=0)
            column_ref[...] = jnp.sum(gates * lane_ref[...], axis=1, keepdims=True)

        @pl.when(at < chunks)
        def _():
            tokens = jnp.concatenate([r[...] for r in token_refs], axis=0)
            gate_acc[...] += jnp.dot(tokens, gate_w[...], preferred_element_type=jnp.float32)
            up_acc[...] += jnp.dot(tokens, up_w[...], preferred_element_type=jnp.float32)

        @pl.when(at == last)
        def _():
            gate = gate_acc[...]
            hidden_ref[...] = (gate / (1.0 + jnp.exp(-gate)) * up_acc[...]).astype(jnp.bfloat16)

        @pl.when(at >= chunks)
        def _():
            outs = jnp.dot(hidden_ref[...], down_w[...], preferred_element_type=jnp.float32)
            outs = (outs * column_ref[...]).astype(jnp.bfloat16)
            for i, out_ref in enumerate(out_refs):
                out_ref[...] = outs[i * rows : (i + 1) * rows]

    def inward(i):
        return jnp.minimum(i, last)

    def outward(i):
        return jnp.maximum(i - chunks, 0)

    return pl.pallas_call(
        body,
        out_shape=[jax.ShapeDtypeStruct((rows, features), jnp.bfloat16)] * count,
        grid=(2 * chunks,),
        in_specs=[pl.BlockSpec((rows, FEATURE_CHUNK), lambda i: (0, inward(i)))] * count
        + [pl.BlockSpec((rows, GATE_LANES), lambda i: (0, features // GATE_LANES))] * count
        + [
            pl.BlockSpec((1, GATE_LANES), lambda i: (0, 0)),
            pl.BlockSpec((FEATURE_CHUNK, hidden_units), lambda i: (inward(i), 0)),
            pl.BlockSpec((FEATURE_CHUNK, hidden_units), lambda i: (inward(i), 0)),
            pl.BlockSpec((hidden_units, FEATURE_CHUNK), lambda i: (0, outward(i))),
        ]
        + [pl.BlockSpec(memory_space=pl.ANY)] * len(after),
        out_specs=[pl.BlockSpec((rows, FEATURE_CHUNK), lambda i: (0, outward(i)))] * count,
        scratch_shapes=[
            pltpu.VMEM((all_rows, hidden_units), jnp.float32),
            pltpu.VMEM((all_rows, hidden_units), jnp.float32),
            pltpu.VMEM((all_rows, hidden_units), jnp.bfloat16),
            pltpu.VMEM((all_rows, 1), jnp.float32),
        ],
        compiler_params=pltpu.CompilerParams(vmem_limit_bytes=EXPERT_VMEM),
        cost_estimate=pl.CostEstimate(
            flops=6 * all_rows * features * hidden_units,
            bytes_accessed=2 * (3 * features * hidden_units + 2 * all_rows * features),
            transcendentals=all_rows * hidden_units,
        ),
        name="experts",
    )(*blocks, *blocks, my_lane, w_gate, w_up, w_down, *after)


def routed_block(
    hidden_state, ffn_gain, expert_ids, expert_gates, w_gate, w_up, w_down, attended
):
    steps, requests, features = hidden_state.shape
    near, middle, far = ("z", "x"), ("y", "z"), ("x", "y")
    own = prepare(hidden_state, ffn_gain, expert_ids, expert_gates)
    own = stack(collect(own, near))
    own = stack(collect(own, middle))
    groups = lax.axis_size(AXES)
    my_expert = lax.axis_index(AXES) // (groups // EXPERTS)
    my_lane = (jnp.arange(GATE_LANES, dtype=jnp.int32) == my_expert).astype(jnp.float32)[None, :]

    def apply_expert(blocks, after):
        both = blocks + [other_core(b) for b in blocks]
        outs = expert_call(both, my_lane, w_gate, w_up, w_down, after)
        return outs[: len(blocks)], [other_core(b) for b in outs[len(blocks) :]]

    def merge(mine, received):
        return [add_up(pair) for pair in zip(mine, received)]

    above, below = shift(own, far, -1), shift(own, far, 1)
    own_out, own_back = apply_expert([own], [attended])
    above, below, own = hold([above, below, own], own_out)
    opposite = shift(own, far, 2)
    above, below = merge(*apply_expert([above, below], own_out))
    near_home = [shift(above, far, 1), shift(below, far, -1)]
    opposite_out, opposite_back = apply_expert([opposite], [above, below])
    opposite_back = hold(opposite_back, near_home)
    far_home = shift(merge(opposite_out, opposite_back)[0], far, 2)
    own = merge(own_out, own_back)[0]
    parts = zip(*[cut(block, SIDE) for block in (own, *near_home, far_home)])
    summed = add_up(send_home([add_up(p) for p in parts], middle))
    summed = add_up(send_home(cut(summed, SIDE), near))
    return summed.reshape(steps, requests, features)


def on_device(
    hidden_state,
    ffn_gain,
    expert_ids,
    expert_gates,
    w_gate,
    w_up,
    w_down,
    queries,
    kv_cache,
    new_keys,
    cache_lengths,
):
    attended = attend(queries, kv_cache, new_keys, cache_lengths)
    routed = routed_block(
        hidden_state, ffn_gain, expert_ids, expert_gates, w_gate, w_up, w_down, attended
    )
    return attended, routed


def solution(mesh):
    chips = Mesh(mesh.devices.reshape(2, SIDE, SIDE, SIDE), AXES)
    placed = (
        P(None, AXES, None),
        P(),
        P(None, AXES, None),
        P(None, AXES, None),
        P(None, AXES),
        P(None, AXES),
        P(AXES, None),
        P(None, AXES, None, None),
        P(AXES, None, None),
        P(None, AXES, None),
        P(AXES),
    )
    return jax.shard_map(
        on_device,
        mesh=chips,
        in_specs=placed,
        out_specs=(P(None, AXES, None, None), P(None, AXES, None)),
        check_vma=False,
    )
```

```python
import functools
import math

import jax
import jax.numpy as jnp
from jax import lax
from jax.experimental import pallas as pl
from jax.experimental.pallas import tpu as pltpu
from jax.sharding import Mesh
from jax.sharding import PartitionSpec as P

KV_RANK = 512
EPS = 1e-06
SCORE_SCALE = 1.0 / math.sqrt(192.0)
AXES = ("c", "y", "z", "x")
SIDE = 4
GATE_LANES = 128
SLOT_CHUNK = 512
FEATURE_CHUNK = 3584
SMALL_VMEM = 4 * 1024 * 1024
ATTEND_VMEM = 16 * 1024 * 1024
JOIN_VMEM = 12 * 1024 * 1024
EXPERT_VMEM = 12 * 1024 * 1024


def device_number(c, y, z, x):
    return ((c * SIDE + y) * SIDE + z) * SIDE + x


def shifted_pairs(axis_of_core, distance):
    pairs = []
    for c in range(2):
        for y in range(SIDE):
            for z in range(SIDE):
                for x in range(SIDE):
                    place = {"y": y, "z": z, "x": x}
                    axis = axis_of_core[c]
                    place[axis] = (place[axis] + distance) % SIDE
                    pairs.append((device_number(c, y, z, x), device_number(c, **place)))
    return pairs


def shift(block, axis_of_core, distance):
    return lax.ppermute(block, AXES, shifted_pairs(axis_of_core, distance))


def other_core(block):
    return lax.ppermute(block, "c", [(0, 1), (1, 0)])


def collect(block, axis_of_core):
    return [
        block,
        shift(block, axis_of_core, -1),
        shift(block, axis_of_core, 1),
        shift(block, axis_of_core, 2),
    ]


def send_home(blocks, axis_of_core):
    return [
        blocks[0],
        shift(blocks[1], axis_of_core, 1),
        shift(blocks[2], axis_of_core, -1),
        shift(blocks[3], axis_of_core, 2),
    ]


def add_up(blocks):
    total = blocks[0].astype(jnp.float32)
    for block in blocks[1:]:
        total = total + block.astype(jnp.float32)
    return total.astype(jnp.bfloat16)


def cut(rows, parts):
    size = rows.shape[0] // parts
    return [rows[i * size : (i + 1) * size] for i in range(parts)]


def prepare_body(state_in, gain_in, id_in, gate_in, out_ref, state_ref, gain_ref, id_ref, gate_ref, sems):
    pairs = ((state_in, state_ref), (gain_in, gain_ref), (id_in, id_ref), (gate_in, gate_ref))
    copies = [pltpu.make_async_copy(a, b, sems.at[i]) for i, (a, b) in enumerate(pairs)]
    for copy in copies:
        copy.start()
    for copy in copies:
        copy.wait()
    steps, requests, features = state_ref.shape
    gain = gain_ref[...].astype(jnp.float32)
    lanes = lax.broadcasted_iota(jnp.int32, (requests, GATE_LANES), 1)
    for s in range(steps):
        rows = pl.ds(s * requests, requests)
        values = state_ref[s].astype(jnp.float32)
        factor = lax.rsqrt(jnp.mean(values * values, axis=-1, keepdims=True) + EPS)
        for j in range(gain.shape[0]):
            at = slice(j * GATE_LANES, (j + 1) * GATE_LANES)
            scaled = values[:, at] * factor * gain[j : j + 1]
            out_ref[rows, at] = scaled.astype(jnp.bfloat16)
        ids, gates = id_ref[s], gate_ref[s].astype(jnp.float32)
        table = jnp.zeros((requests, GATE_LANES), jnp.float32)
        for k in range(ids.shape[1]):
            table = table + jnp.where(lanes == ids[:, k : k + 1], gates[:, k : k + 1], 0.0)
        out_ref[rows, features:] = table.astype(jnp.bfloat16)


def prepare(hidden_state, ffn_gain, expert_ids, expert_gates):
    steps, requests, features = hidden_state.shape
    inputs = (hidden_state, ffn_gain.reshape(-1, GATE_LANES), expert_ids, expert_gates)
    inputs = [in_hbm(a) for a in inputs]
    return pl.pallas_call(
        prepare_body,
        out_shape=jax.ShapeDtypeStruct((steps * requests, features + GATE_LANES), jnp.bfloat16),
        in_specs=[pl.BlockSpec(memory_space=pltpu.HBM)] * len(inputs),
        scratch_shapes=[pltpu.VMEM(a.shape, a.dtype) for a in inputs]
        + [pltpu.SemaphoreType.DMA((len(inputs),))],
        compiler_params=pltpu.CompilerParams(vmem_limit_bytes=SMALL_VMEM),
        name="prepare",
    )(*inputs)


def in_hbm(array):
    return pltpu.with_memory_space_constraint(array, pltpu.HBM)


def stack_body(*refs):
    rows = refs[0].shape[0]
    for i, ref in enumerate(refs[:-1]):
        refs[-1][pl.ds(i * rows, rows), :] = ref[...]


def stack(blocks):
    if len(blocks) == 1:
        return blocks[0]
    rows, width = blocks[0].shape
    return pl.pallas_call(
        stack_body,
        out_shape=jax.ShapeDtypeStruct((rows * len(blocks), width), blocks[0].dtype),
        compiler_params=pltpu.CompilerParams(vmem_limit_bytes=SMALL_VMEM),
        name="stack",
    )(*blocks)


def attend_body(length_ref, q_ref, k_ref, fresh_ref, out_ref, score_ref):
    request = pl.program_id(0)
    length = length_ref[request]
    steps, heads = q_ref.shape[0], q_ref.shape[3]
    slots = k_ref.shape[2]
    q = jnp.concatenate([q_ref[s, 0].T for s in range(steps)], axis=0)
    fresh = fresh_ref[0]
    fresh_scores = (
        lax.dot_general(q, fresh, (((1,), (1,)), ((), ())), preferred_element_type=jnp.float32)
        * SCORE_SCALE
    )
    row_step = lax.broadcasted_iota(jnp.int32, fresh_scores.shape, 0) // heads
    fresh_lane = lax.broadcasted_iota(jnp.int32, fresh_scores.shape, 1)
    fresh_scores = jnp.where(fresh_lane <= row_step, fresh_scores, -jnp.inf)
    top = jnp.max(fresh_scores, axis=1, keepdims=True)
    for start in range(0, slots, SLOT_CHUNK):
        cols = pl.ds(start, SLOT_CHUNK)
        scores = jnp.dot(q, k_ref[0, :, cols], preferred_element_type=jnp.float32) * SCORE_SCALE
        slot = lax.broadcasted_iota(jnp.int32, scores.shape, 1) + start
        scores = jnp.where(slot < length, scores, -jnp.inf)
        score_ref[:, cols] = scores
        top = jnp.maximum(top, jnp.max(scores, axis=1, keepdims=True))
    fresh_exp = jnp.exp(fresh_scores - top)
    denominator = jnp.sum(fresh_exp, axis=1, keepdims=True)
    total = jnp.dot(
        fresh_exp.astype(jnp.bfloat16), fresh[:, :KV_RANK], preferred_element_type=jnp.float32
    )
    for start in range(0, slots, SLOT_CHUNK):
        cols = pl.ds(start, SLOT_CHUNK)
        weights = jnp.exp(score_ref[:, cols] - top)
        denominator = denominator + jnp.sum(weights, axis=1, keepdims=True)
        total = total + lax.dot_general(
            weights.astype(jnp.bfloat16),
            k_ref[0, :KV_RANK, cols],
            (((1,), (1,)), ((), ())),
            preferred_element_type=jnp.float32,
        )
    result = (total / denominator).astype(jnp.bfloat16)
    for s in range(steps):
        out_ref[s, 0] = result[s * heads : (s + 1) * heads]


def attend(queries, kv_cache, new_keys, cache_lengths):
    steps, requests, heads, width = queries.shape
    slots = kv_cache.shape[1]
    q_t = jnp.swapaxes(queries, 2, 3)
    k_t = jnp.swapaxes(kv_cache, 1, 2)
    fresh = jnp.pad(jnp.swapaxes(new_keys, 0, 1), ((0, 0), (0, 16 - steps), (0, 0)))
    return pl.pallas_call(
        attend_body,
        out_shape=jax.ShapeDtypeStruct((steps, requests, heads, KV_RANK), jnp.bfloat16),
        grid=(requests,),
        in_specs=[
            pl.BlockSpec(memory_space=pltpu.SMEM),
            pl.BlockSpec((steps, 1, width, heads), lambda r: (0, r, 0, 0)),
            pl.BlockSpec((1, width, slots), lambda r: (r, 0, 0)),
            pl.BlockSpec((1, 16, width), lambda r: (r, 0, 0)),
        ],
        out_specs=pl.BlockSpec((steps, 1, heads, KV_RANK), lambda r: (0, r, 0, 0)),
        scratch_shapes=[pltpu.VMEM((steps * heads, slots), jnp.float32)],
        compiler_params=pltpu.CompilerParams(vmem_limit_bytes=ATTEND_VMEM),
        cost_estimate=pl.CostEstimate(
            flops=2 * steps * requests * heads * slots * (width + KV_RANK),
            bytes_accessed=2 * requests * (slots * width + steps * heads * (width + KV_RANK)),
            transcendentals=steps * requests * heads * slots,
        ),
        name="attend",
    )(cache_lengths, in_hbm(q_t), in_hbm(k_t), fresh)


def join_body(*refs):
    in_refs, out_refs = refs[:-SIDE], refs[-SIDE:]
    half = len(in_refs) // 2
    mine, back = (
        jnp.concatenate([r[...].astype(jnp.float32) for r in part], axis=0)
        for part in (in_refs[:half], in_refs[half:])
    )
    total = (mine + back).astype(jnp.bfloat16)
    for out_ref, piece in zip(out_refs, cut(total, SIDE)):
        out_ref[...] = piece


def join(mine, back):
    rows, width = sum(b.shape[0] for b in back), back[0].shape[1]
    piece = jax.ShapeDtypeStruct((rows // SIDE, width), back[0].dtype)
    return pl.pallas_call(
        join_body,
        out_shape=[piece] * SIDE,
        compiler_params=pltpu.CompilerParams(vmem_limit_bytes=JOIN_VMEM),
        name="join",
    )(*mine, *back)


def hold_body(*refs):
    pass


def hold(blocks, after):
    anywhere = pl.BlockSpec(memory_space=pl.ANY)
    return pl.pallas_call(
        hold_body,
        out_shape=[jax.ShapeDtypeStruct(b.shape, b.dtype) for b in blocks],
        in_specs=[anywhere] * (len(blocks) + len(after)),
        out_specs=[anywhere] * len(blocks),
        input_output_aliases={i: i for i in range(len(blocks))},
        compiler_params=pltpu.CompilerParams(vmem_limit_bytes=1024 * 1024),
        name="hold",
    )(*blocks, *after)


def resident_body(*refs, count):
    sems, outs = refs[-1], refs[-1 - count : -1]
    copies = [pltpu.make_async_copy(refs[i], outs[i], sems.at[i]) for i in range(count)]
    for copy in copies:
        copy.start()
    for copy in copies:
        copy.wait()


def resident(weights, after):
    count = len(weights)
    return pl.pallas_call(
        functools.partial(resident_body, count=count),
        out_shape=[pltpu.VMEM(w.shape, w.dtype) for w in weights],
        in_specs=[pl.BlockSpec(memory_space=pltpu.HBM)] * count
        + [pl.BlockSpec(memory_space=pl.ANY)] * len(after),
        out_specs=[pl.BlockSpec(memory_space=pltpu.VMEM)] * count,
        scratch_shapes=[pltpu.SemaphoreType.DMA((count,))],
        compiler_params=pltpu.CompilerParams(vmem_limit_bytes=SMALL_VMEM),
        name="resident",
    )(*[in_hbm(w) for w in weights], *after)


def expert_call(blocks, weights, after):
    count = len(blocks)
    heights = [b.shape[0] for b in blocks]
    features, hidden_units = weights[0].shape
    chunks = features // FEATURE_CHUNK
    last = chunks - 1
    all_rows = sum(heights)
    first_out = 2 * count + 3 + len(after)

    def body(*refs):
        token_refs, gate_refs = refs[:count], refs[count : 2 * count]
        gate_w, up_w, down_w = refs[2 * count : 2 * count + 3]
        out_refs = refs[first_out : first_out + count]
        gate_acc, up_acc, hidden_ref, column_ref = refs[first_out + count :]
        at = pl.program_id(0)

        @pl.when(at == 0)
        def _():
            gates = jnp.concatenate([r[...].astype(jnp.float32) for r in gate_refs], axis=0)
            core, y, z = (lax.axis_index(name) for name in ("c", "y", "z"))
            expert = (core * SIDE + y) * 2 + (z >= SIDE // 2).astype(jnp.int32)
            lanes = lax.broadcasted_iota(jnp.int32, gates.shape, 1)
            picked = jnp.where(lanes == expert, gates, 0.0)
            column_ref[...] = jnp.sum(picked, axis=1, keepdims=True)

        for step in range(chunks):
            here = pl.ds(step * FEATURE_CHUNK, FEATURE_CHUNK)

            @pl.when(at == step)
            def _():
                tokens = jnp.concatenate([r[...] for r in token_refs], axis=0)
                gate = jnp.dot(tokens, gate_w[here, :], preferred_element_type=jnp.float32)
                up = jnp.dot(tokens, up_w[here, :], preferred_element_type=jnp.float32)
                if step:
                    gate, up = gate + gate_acc[...], up + up_acc[...]
                if step < last:
                    gate_acc[...], up_acc[...] = gate, up
                else:
                    hidden = gate / (1.0 + jnp.exp(-gate)) * up
                    hidden_ref[...] = hidden.astype(jnp.bfloat16)

            @pl.when(at == chunks + step)
            def _():
                outs = jnp.dot(hidden_ref[...], down_w[:, here], preferred_element_type=jnp.float32)
                outs = (outs * column_ref[...]).astype(jnp.bfloat16)
                top = 0
                for out_ref, height in zip(out_refs, heights):
                    out_ref[...] = outs[top : top + height]
                    top += height

    def inward(i):
        return jnp.minimum(i, last)

    def outward(i):
        return jnp.maximum(i - chunks, 0)

    return pl.pallas_call(
        body,
        out_shape=[jax.ShapeDtypeStruct((h, features), jnp.bfloat16) for h in heights],
        grid=(2 * chunks,),
        in_specs=[pl.BlockSpec((h, FEATURE_CHUNK), lambda i: (0, inward(i))) for h in heights]
        + [pl.BlockSpec((h, GATE_LANES), lambda i: (0, features // GATE_LANES)) for h in heights]
        + [pl.BlockSpec(memory_space=pltpu.VMEM)] * 3
        + [pl.BlockSpec(memory_space=pl.ANY)] * len(after),
        out_specs=[pl.BlockSpec((h, FEATURE_CHUNK), lambda i: (0, outward(i))) for h in heights],
        scratch_shapes=[
            pltpu.VMEM((all_rows, hidden_units), jnp.float32),
            pltpu.VMEM((all_rows, hidden_units), jnp.float32),
            pltpu.VMEM((all_rows, hidden_units), jnp.bfloat16),
            pltpu.VMEM((all_rows, 1), jnp.float32),
        ],
        compiler_params=pltpu.CompilerParams(vmem_limit_bytes=EXPERT_VMEM),
        cost_estimate=pl.CostEstimate(
            flops=6 * all_rows * features * hidden_units,
            bytes_accessed=4 * all_rows * features,
            transcendentals=all_rows * hidden_units,
        ),
        name="experts",
    )(*blocks, *blocks, *weights, *after)


def routed_block(
    hidden_state, ffn_gain, expert_ids, expert_gates, w_gate, w_up, w_down, attended
):
    steps, requests, features = hidden_state.shape
    near, middle, far = ("z", "x"), ("y", "z"), ("x", "y")
    own = prepare(hidden_state, ffn_gain, expert_ids, expert_gates)
    own = stack(collect(own, near))
    pieces = collect(own, middle)
    first, second = stack(pieces[:2]), stack(pieces[2:])

    def apply_expert(blocks, after):
        theirs = other_core(stack(blocks))
        *mine, theirs = expert_call([*blocks, theirs], weights, after)
        return mine, other_core(theirs)

    def merge(mine, received):
        return [add_up(pair) for pair in zip(mine, cut(received, len(mine)))]

    def neighbours(block):
        return [shift(block, far, -1), shift(block, far, 1)]

    arrived = neighbours(first) + neighbours(second)
    weights = resident([w_gate, w_up, w_down], [in_hbm(attended), *arrived[:2]])
    own, *arrived = hold([stack([first, second]), *arrived], weights)
    opposite = [shift(arrived[0], far, -1), shift(arrived[3], far, 1)]
    outs, back = apply_expert(arrived[:2], [])
    sums = merge(outs, back)
    outs, back = apply_expert(arrived[2:], outs[:1])
    sums += merge(outs, back)
    home = [shift(stack(sums[0::2]), far, 1), shift(stack(sums[1::2]), far, -1)]
    own_out, own_back = apply_expert([own], outs[:1])
    opposite = hold(opposite, [*sums, *own_out])
    theirs = [other_core(block) for block in opposite]
    outs = expert_call([*opposite, *theirs], weights, own_out)
    back = [other_core(block) for block in outs[2:]]
    own_sum = add_up([own_out[0], own_back])
    back = hold(back, [*home, own_back])
    far_sum = add_up(send_home(join(outs[:2], back), middle))
    far_sum = shift(far_sum, far, 2)
    blocks = [cut(block, SIDE) for block in (own_sum, *home)]
    summed = send_home([add_up(p) for p in zip(*blocks)], middle)
    summed = add_up([*summed, far_sum])
    summed = add_up(send_home(cut(summed, SIDE), near))
    return summed.reshape(steps, requests, features)


def on_device(
    hidden_state,
    ffn_gain,
    expert_ids,
    expert_gates,
    w_gate,
    w_up,
    w_down,
    queries,
    kv_cache,
    new_keys,
    cache_lengths,
):
    attended = attend(queries, kv_cache, new_keys, cache_lengths)
    routed = routed_block(
        hidden_state, ffn_gain, expert_ids, expert_gates, w_gate, w_up, w_down, attended
    )
    return attended, routed


def solution(mesh):
    chips = Mesh(mesh.devices.reshape(2, SIDE, SIDE, SIDE), AXES)
    placed = (
        P(None, AXES, None),
        P(),
        P(None, AXES, None),
        P(None, AXES, None),
        P(None, AXES),
        P(None, AXES),
        P(AXES, None),
        P(None, AXES, None, None),
        P(AXES, None, None),
        P(None, AXES, None),
        P(AXES),
    )
    return jax.shard_map(
        on_device,
        mesh=chips,
        in_specs=placed,
        out_specs=(P(None, AXES, None, None), P(None, AXES, None)),
        check_vma=False,
    )
```

```python
import functools
import math

import jax
import jax.numpy as jnp
from jax import lax
from jax.experimental import pallas as pl
from jax.experimental.pallas import tpu as pltpu
from jax.sharding import Mesh
from jax.sharding import PartitionSpec as P

KV_RANK = 512
EPS = 1e-06
SCORE_SCALE = 1.0 / math.sqrt(192.0)
AXES = ("c", "y", "z", "x")
SIDE = 4
GATE_LANES = 128
SLOT_CHUNK = 512
FEATURE_CHUNK = 1792
SMALL_VMEM = 4 * 1024 * 1024
ATTEND_VMEM = 16 * 1024 * 1024
JOIN_VMEM = 12 * 1024 * 1024
EXPERT_VMEM = 12 * 1024 * 1024


def device_number(c, y, z, x):
    return ((c * SIDE + y) * SIDE + z) * SIDE + x


def shifted_pairs(axis_of_core, distance):
    pairs = []
    for c in range(2):
        for y in range(SIDE):
            for z in range(SIDE):
                for x in range(SIDE):
                    place = {"y": y, "z": z, "x": x}
                    axis = axis_of_core[c]
                    place[axis] = (place[axis] + distance) % SIDE
                    pairs.append((device_number(c, y, z, x), device_number(c, **place)))
    return pairs


def shift(block, axis_of_core, distance):
    return lax.ppermute(block, AXES, shifted_pairs(axis_of_core, distance))


def other_core(block):
    return lax.ppermute(block, "c", [(0, 1), (1, 0)])


def collect(block, axis_of_core):
    return [
        block,
        shift(block, axis_of_core, -1),
        shift(block, axis_of_core, 1),
        shift(block, axis_of_core, 2),
    ]


def send_home(blocks, axis_of_core):
    return [
        blocks[0],
        shift(blocks[1], axis_of_core, 1),
        shift(blocks[2], axis_of_core, -1),
        shift(blocks[3], axis_of_core, 2),
    ]


def add_up(blocks):
    total = blocks[0].astype(jnp.float32)
    for block in blocks[1:]:
        total = total + block.astype(jnp.float32)
    return total.astype(jnp.bfloat16)


def cut(rows, parts):
    size = rows.shape[0] // parts
    return [rows[i * size : (i + 1) * size] for i in range(parts)]


def prepare_body(state_in, gain_in, id_in, gate_in, out_ref, state_ref, gain_ref, id_ref, gate_ref, sems):
    pairs = ((state_in, state_ref), (gain_in, gain_ref), (id_in, id_ref), (gate_in, gate_ref))
    copies = [pltpu.make_async_copy(a, b, sems.at[i]) for i, (a, b) in enumerate(pairs)]
    for copy in copies:
        copy.start()
    for copy in copies:
        copy.wait()
    steps, requests, features = state_ref.shape
    gain = gain_ref[...].astype(jnp.float32)
    lanes = lax.broadcasted_iota(jnp.int32, (requests, GATE_LANES), 1)
    for s in range(steps):
        rows = pl.ds(s * requests, requests)
        values = state_ref[s].astype(jnp.float32)
        factor = lax.rsqrt(jnp.mean(values * values, axis=-1, keepdims=True) + EPS)
        for j in range(gain.shape[0]):
            at = slice(j * GATE_LANES, (j + 1) * GATE_LANES)
            scaled = values[:, at] * factor * gain[j : j + 1]
            out_ref[rows, at] = scaled.astype(jnp.bfloat16)
        ids, gates = id_ref[s], gate_ref[s].astype(jnp.float32)
        table = jnp.zeros((requests, GATE_LANES), jnp.float32)
        for k in range(ids.shape[1]):
            table = table + jnp.where(lanes == ids[:, k : k + 1], gates[:, k : k + 1], 0.0)
        out_ref[rows, features:] = table.astype(jnp.bfloat16)


def prepare(hidden_state, ffn_gain, expert_ids, expert_gates):
    steps, requests, features = hidden_state.shape
    inputs = (hidden_state, ffn_gain.reshape(-1, GATE_LANES), expert_ids, expert_gates)
    inputs = [in_hbm(a) for a in inputs]
    return pl.pallas_call(
        prepare_body,
        out_shape=jax.ShapeDtypeStruct((steps * requests, features + GATE_LANES), jnp.bfloat16),
        in_specs=[pl.BlockSpec(memory_space=pltpu.HBM)] * len(inputs),
        scratch_shapes=[pltpu.VMEM(a.shape, a.dtype) for a in inputs]
        + [pltpu.SemaphoreType.DMA((len(inputs),))],
        compiler_params=pltpu.CompilerParams(vmem_limit_bytes=SMALL_VMEM),
        name="prepare",
    )(*inputs)


def in_hbm(array):
    return pltpu.with_memory_space_constraint(array, pltpu.HBM)


def stack_body(*refs):
    rows = refs[0].shape[0]
    for i, ref in enumerate(refs[:-1]):
        refs[-1][pl.ds(i * rows, rows), :] = ref[...]


def stack(blocks):
    if len(blocks) == 1:
        return blocks[0]
    rows, width = blocks[0].shape
    return pl.pallas_call(
        stack_body,
        out_shape=jax.ShapeDtypeStruct((rows * len(blocks), width), blocks[0].dtype),
        compiler_params=pltpu.CompilerParams(vmem_limit_bytes=SMALL_VMEM),
        name="stack",
    )(*blocks)


def attend_body(length_ref, q_ref, k_ref, fresh_ref, out_ref, score_ref):
    request = pl.program_id(0)
    length = length_ref[request]
    steps, heads = q_ref.shape[0], q_ref.shape[3]
    slots = k_ref.shape[2]
    q = jnp.concatenate([q_ref[s, 0].T for s in range(steps)], axis=0)
    fresh = fresh_ref[0]
    fresh_scores = (
        lax.dot_general(q, fresh, (((1,), (1,)), ((), ())), preferred_element_type=jnp.float32)
        * SCORE_SCALE
    )
    row_step = lax.broadcasted_iota(jnp.int32, fresh_scores.shape, 0) // heads
    fresh_lane = lax.broadcasted_iota(jnp.int32, fresh_scores.shape, 1)
    fresh_scores = jnp.where(fresh_lane <= row_step, fresh_scores, -jnp.inf)
    top = jnp.max(fresh_scores, axis=1, keepdims=True)
    for start in range(0, slots, SLOT_CHUNK):
        cols = pl.ds(start, SLOT_CHUNK)
        scores = jnp.dot(q, k_ref[0, :, cols], preferred_element_type=jnp.float32) * SCORE_SCALE
        slot = lax.broadcasted_iota(jnp.int32, scores.shape, 1) + start
        scores = jnp.where(slot < length, scores, -jnp.inf)
        score_ref[:, cols] = scores
        top = jnp.maximum(top, jnp.max(scores, axis=1, keepdims=True))
    fresh_exp = jnp.exp(fresh_scores - top)
    denominator = jnp.sum(fresh_exp, axis=1, keepdims=True)
    total = jnp.dot(
        fresh_exp.astype(jnp.bfloat16), fresh[:, :KV_RANK], preferred_element_type=jnp.float32
    )
    for start in range(0, slots, SLOT_CHUNK):
        cols = pl.ds(start, SLOT_CHUNK)
        weights = jnp.exp(score_ref[:, cols] - top)
        denominator = denominator + jnp.sum(weights, axis=1, keepdims=True)
        total = total + lax.dot_general(
            weights.astype(jnp.bfloat16),
            k_ref[0, :KV_RANK, cols],
            (((1,), (1,)), ((), ())),
            preferred_element_type=jnp.float32,
        )
    result = (total / denominator).astype(jnp.bfloat16)
    for s in range(steps):
        out_ref[s, 0] = result[s * heads : (s + 1) * heads]


def attend(queries, kv_cache, new_keys, cache_lengths):
    steps, requests, heads, width = queries.shape
    slots = kv_cache.shape[1]
    q_t = jnp.swapaxes(queries, 2, 3)
    k_t = jnp.swapaxes(kv_cache, 1, 2)
    fresh = jnp.pad(jnp.swapaxes(new_keys, 0, 1), ((0, 0), (0, 16 - steps), (0, 0)))
    return pl.pallas_call(
        attend_body,
        out_shape=jax.ShapeDtypeStruct((steps, requests, heads, KV_RANK), jnp.bfloat16),
        grid=(requests,),
        in_specs=[
            pl.BlockSpec(memory_space=pltpu.SMEM),
            pl.BlockSpec((steps, 1, width, heads), lambda r: (0, r, 0, 0)),
            pl.BlockSpec((1, width, slots), lambda r: (r, 0, 0)),
            pl.BlockSpec((1, 16, width), lambda r: (r, 0, 0)),
        ],
        out_specs=pl.BlockSpec((steps, 1, heads, KV_RANK), lambda r: (0, r, 0, 0)),
        scratch_shapes=[pltpu.VMEM((steps * heads, slots), jnp.float32)],
        compiler_params=pltpu.CompilerParams(vmem_limit_bytes=ATTEND_VMEM),
        cost_estimate=pl.CostEstimate(
            flops=2 * steps * requests * heads * slots * (width + KV_RANK),
            bytes_accessed=2 * requests * (slots * width + steps * heads * (width + KV_RANK)),
            transcendentals=steps * requests * heads * slots,
        ),
        name="attend",
    )(cache_lengths, in_hbm(q_t), in_hbm(k_t), fresh)


def join_body(*refs):
    in_refs, out_refs = refs[:-SIDE], refs[-SIDE:]
    half = len(in_refs) // 2
    mine, back = (
        jnp.concatenate([r[...].astype(jnp.float32) for r in part], axis=0)
        for part in (in_refs[:half], in_refs[half:])
    )
    total = (mine + back).astype(jnp.bfloat16)
    for out_ref, piece in zip(out_refs, cut(total, SIDE)):
        out_ref[...] = piece


def join(mine, back):
    rows, width = sum(b.shape[0] for b in back), back[0].shape[1]
    piece = jax.ShapeDtypeStruct((rows // SIDE, width), back[0].dtype)
    return pl.pallas_call(
        join_body,
        out_shape=[piece] * SIDE,
        compiler_params=pltpu.CompilerParams(vmem_limit_bytes=JOIN_VMEM),
        name="join",
    )(*mine, *back)


def hold_body(*refs):
    pass


def hold(blocks, after):
    anywhere = pl.BlockSpec(memory_space=pl.ANY)
    return pl.pallas_call(
        hold_body,
        out_shape=[jax.ShapeDtypeStruct(b.shape, b.dtype) for b in blocks],
        in_specs=[anywhere] * (len(blocks) + len(after)),
        out_specs=[anywhere] * len(blocks),
        input_output_aliases={i: i for i in range(len(blocks))},
        compiler_params=pltpu.CompilerParams(vmem_limit_bytes=1024 * 1024),
        name="hold",
    )(*blocks, *after)


def resident_body(*refs, count):
    sems, outs = refs[-1], refs[-1 - count : -1]
    copies = [pltpu.make_async_copy(refs[i], outs[i], sems.at[i]) for i in range(count)]
    for copy in copies:
        copy.start()
    for copy in copies:
        copy.wait()


def resident(weights, after):
    count = len(weights)
    return pl.pallas_call(
        functools.partial(resident_body, count=count),
        out_shape=[pltpu.VMEM(w.shape, w.dtype) for w in weights],
        in_specs=[pl.BlockSpec(memory_space=pltpu.HBM)] * count
        + [pl.BlockSpec(memory_space=pl.ANY)] * len(after),
        out_specs=[pl.BlockSpec(memory_space=pltpu.VMEM)] * count,
        scratch_shapes=[pltpu.SemaphoreType.DMA((count,))],
        compiler_params=pltpu.CompilerParams(vmem_limit_bytes=SMALL_VMEM),
        name="resident",
    )(*[in_hbm(w) for w in weights], *after)


def expert_body(*refs, count):
    token_refs = refs[:count]
    gate_w, up_w, down_w = refs[count : count + 3]
    out_refs = refs[-count:]
    features = gate_w.shape[0]
    heights = [r.shape[0] for r in token_refs]

    def tokens(at):
        return jnp.concatenate([r[:, at] for r in token_refs], axis=0)

    gates = tokens(pl.ds(features, GATE_LANES)).astype(jnp.float32)
    core, y, z = (lax.axis_index(name) for name in ("c", "y", "z"))
    expert = (core * SIDE + y) * 2 + (z >= SIDE // 2).astype(jnp.int32)
    lanes = lax.broadcasted_iota(jnp.int32, gates.shape, 1)
    column = jnp.sum(jnp.where(lanes == expert, gates, 0.0), axis=1, keepdims=True)

    chunks = [pl.ds(i, FEATURE_CHUNK) for i in range(0, features, FEATURE_CHUNK)]
    gate = up = None
    for at in chunks:
        rows = tokens(at)
        more_gate = jnp.dot(rows, gate_w[at, :], preferred_element_type=jnp.float32)
        more_up = jnp.dot(rows, up_w[at, :], preferred_element_type=jnp.float32)
        gate = more_gate if gate is None else gate + more_gate
        up = more_up if up is None else up + more_up
    hidden = (gate / (1.0 + jnp.exp(-gate)) * up).astype(jnp.bfloat16)
    for at in chunks:
        outs = jnp.dot(hidden, down_w[:, at], preferred_element_type=jnp.float32)
        outs = (outs * column).astype(jnp.bfloat16)
        top = 0
        for out_ref, height in zip(out_refs, heights):
            out_ref[:, at] = outs[top : top + height]
            top += height


def expert_call(blocks, weights, after):
    count = len(blocks)
    heights = [b.shape[0] for b in blocks]
    all_rows = sum(heights)
    features, hidden_units = weights[0].shape
    whole = pl.BlockSpec(memory_space=pltpu.VMEM)
    return pl.pallas_call(
        functools.partial(expert_body, count=count),
        out_shape=[jax.ShapeDtypeStruct((h, features), jnp.bfloat16) for h in heights],
        in_specs=[whole] * (count + 3) + [pl.BlockSpec(memory_space=pl.ANY)] * len(after),
        out_specs=[whole] * count,
        compiler_params=pltpu.CompilerParams(vmem_limit_bytes=EXPERT_VMEM),
        cost_estimate=pl.CostEstimate(
            flops=6 * all_rows * features * hidden_units,
            bytes_accessed=4 * all_rows * features,
            transcendentals=all_rows * hidden_units,
        ),
        name="experts",
    )(*blocks, *weights, *after)


def routed_block(
    hidden_state, ffn_gain, expert_ids, expert_gates, w_gate, w_up, w_down, attended
):
    steps, requests, features = hidden_state.shape
    near, middle, far = ("z", "x"), ("y", "z"), ("x", "y")
    own = prepare(hidden_state, ffn_gain, expert_ids, expert_gates)
    own = stack(collect(own, near))
    pieces = collect(own, middle)
    first, second = stack(pieces[:2]), stack(pieces[2:])

    def apply_expert(blocks, after):
        theirs = other_core(stack(blocks))
        *mine, theirs = expert_call([*blocks, theirs], weights, after)
        return mine, other_core(theirs)

    def merge(mine, received):
        return [add_up(pair) for pair in zip(mine, cut(received, len(mine)))]

    def neighbours(block):
        return [shift(block, far, -1), shift(block, far, 1)]

    arrived = neighbours(first) + neighbours(second)
    weights = resident([w_gate, w_up, w_down], [in_hbm(attended), *arrived[:2]])
    own, *arrived = hold([stack([first, second]), *arrived], weights)
    opposite = [shift(arrived[0], far, -1), shift(arrived[3], far, 1)]
    outs, back = apply_expert(arrived[:2], [])
    sums = merge(outs, back)
    outs, back = apply_expert(arrived[2:], outs[:1])
    sums += merge(outs, back)
    home = [shift(stack(sums[0::2]), far, 1), shift(stack(sums[1::2]), far, -1)]
    own_out, own_back = apply_expert([own], outs[:1])
    opposite = hold(opposite, [*sums, *own_out])
    theirs = [other_core(block) for block in opposite]
    outs = expert_call([*opposite, *theirs], weights, own_out)
    back = [other_core(block) for block in hold(outs[2:], [*home, own_back])]
    own_sum = add_up([own_out[0], own_back])
    far_sum = add_up(send_home(join(outs[:2], back), middle))
    far_sum = shift(far_sum, far, 2)
    blocks = [cut(block, SIDE) for block in (own_sum, *home)]
    summed = send_home([add_up(p) for p in zip(*blocks)], middle)
    summed = add_up([*summed, far_sum])
    summed = add_up(send_home(cut(summed, SIDE), near))
    return summed.reshape(steps, requests, features)


def on_device(
    hidden_state,
    ffn_gain,
    expert_ids,
    expert_gates,
    w_gate,
    w_up,
    w_down,
    queries,
    kv_cache,
    new_keys,
    cache_lengths,
):
    attended = attend(queries, kv_cache, new_keys, cache_lengths)
    routed = routed_block(
        hidden_state, ffn_gain, expert_ids, expert_gates, w_gate, w_up, w_down, attended
    )
    return attended, routed


def solution(mesh):
    chips = Mesh(mesh.devices.reshape(2, SIDE, SIDE, SIDE), AXES)
    placed = (
        P(None, AXES, None),
        P(),
        P(None, AXES, None),
        P(None, AXES, None),
        P(None, AXES),
        P(None, AXES),
        P(AXES, None),
        P(None, AXES, None, None),
        P(AXES, None, None),
        P(None, AXES, None),
        P(AXES),
    )
    return jax.shard_map(
        on_device,
        mesh=chips,
        in_specs=placed,
        out_specs=(P(None, AXES, None, None), P(None, AXES, None)),
        check_vma=False,
    )
```

```python
import functools
import math

import jax
import jax.numpy as jnp
from jax import lax
from jax.experimental import pallas as pl
from jax.experimental.pallas import tpu as pltpu
from jax.sharding import Mesh
from jax.sharding import PartitionSpec as P

KV_RANK = 512
EPS = 1e-06
SCORE_SCALE = 1.0 / math.sqrt(192.0)
AXES = ("c", "y", "z", "x")
SIDE = 4
GATE_LANES = 128
SLOT_CHUNK = 512
FEATURE_CHUNK = 1792
SMALL_VMEM = 4 * 1024 * 1024
ATTEND_VMEM = 16 * 1024 * 1024
JOIN_VMEM = 12 * 1024 * 1024
EXPERT_VMEM = 12 * 1024 * 1024


def device_number(c, y, z, x):
    return ((c * SIDE + y) * SIDE + z) * SIDE + x


def shifted_pairs(axis_of_core, distance):
    pairs = []
    for c in range(2):
        for y in range(SIDE):
            for z in range(SIDE):
                for x in range(SIDE):
                    place = {"y": y, "z": z, "x": x}
                    axis = axis_of_core[c]
                    place[axis] = (place[axis] + distance) % SIDE
                    pairs.append((device_number(c, y, z, x), device_number(c, **place)))
    return pairs


def shift(block, axis_of_core, distance):
    return lax.ppermute(block, AXES, shifted_pairs(axis_of_core, distance))


def other_core(block):
    return lax.ppermute(block, "c", [(0, 1), (1, 0)])


def collect(block, axis_of_core):
    return [
        block,
        shift(block, axis_of_core, -1),
        shift(block, axis_of_core, 1),
        shift(block, axis_of_core, 2),
    ]


def send_home(blocks, axis_of_core):
    return [
        blocks[0],
        shift(blocks[1], axis_of_core, 1),
        shift(blocks[2], axis_of_core, -1),
        shift(blocks[3], axis_of_core, 2),
    ]


def add_up(blocks):
    total = blocks[0].astype(jnp.float32)
    for block in blocks[1:]:
        total = total + block.astype(jnp.float32)
    return total.astype(jnp.bfloat16)


def cut(rows, parts):
    size = rows.shape[0] // parts
    return [rows[i * size : (i + 1) * size] for i in range(parts)]


def prepare_body(state_in, gain_in, id_in, gate_in, out_ref, state_ref, gain_ref, id_ref, gate_ref, sems):
    pairs = ((state_in, state_ref), (gain_in, gain_ref), (id_in, id_ref), (gate_in, gate_ref))
    copies = [pltpu.make_async_copy(a, b, sems.at[i]) for i, (a, b) in enumerate(pairs)]
    for copy in copies:
        copy.start()
    for copy in copies:
        copy.wait()
    steps, requests, features = state_ref.shape
    gain = gain_ref[...].astype(jnp.float32)
    lanes = lax.broadcasted_iota(jnp.int32, (requests, GATE_LANES), 1)
    for s in range(steps):
        rows = pl.ds(s * requests, requests)
        values = state_ref[s].astype(jnp.float32)
        factor = lax.rsqrt(jnp.mean(values * values, axis=-1, keepdims=True) + EPS)
        for j in range(gain.shape[0]):
            at = slice(j * GATE_LANES, (j + 1) * GATE_LANES)
            scaled = values[:, at] * factor * gain[j : j + 1]
            out_ref[rows, at] = scaled.astype(jnp.bfloat16)
        ids, gates = id_ref[s], gate_ref[s].astype(jnp.float32)
        table = jnp.zeros((requests, GATE_LANES), jnp.float32)
        for k in range(ids.shape[1]):
            table = table + jnp.where(lanes == ids[:, k : k + 1], gates[:, k : k + 1], 0.0)
        out_ref[rows, features:] = table.astype(jnp.bfloat16)


def prepare(hidden_state, ffn_gain, expert_ids, expert_gates):
    steps, requests, features = hidden_state.shape
    inputs = (hidden_state, ffn_gain.reshape(-1, GATE_LANES), expert_ids, expert_gates)
    inputs = [in_hbm(a) for a in inputs]
    return pl.pallas_call(
        prepare_body,
        out_shape=jax.ShapeDtypeStruct((steps * requests, features + GATE_LANES), jnp.bfloat16),
        in_specs=[pl.BlockSpec(memory_space=pltpu.HBM)] * len(inputs),
        scratch_shapes=[pltpu.VMEM(a.shape, a.dtype) for a in inputs]
        + [pltpu.SemaphoreType.DMA((len(inputs),))],
        compiler_params=pltpu.CompilerParams(vmem_limit_bytes=SMALL_VMEM),
        name="prepare",
    )(*inputs)


def in_hbm(array):
    return pltpu.with_memory_space_constraint(array, pltpu.HBM)


def stack_body(*refs):
    rows = refs[0].shape[0]
    for i, ref in enumerate(refs[:-1]):
        refs[-1][pl.ds(i * rows, rows), :] = ref[...]


def stack(blocks):
    if len(blocks) == 1:
        return blocks[0]
    rows, width = blocks[0].shape
    return pl.pallas_call(
        stack_body,
        out_shape=jax.ShapeDtypeStruct((rows * len(blocks), width), blocks[0].dtype),
        compiler_params=pltpu.CompilerParams(vmem_limit_bytes=SMALL_VMEM),
        name="stack",
    )(*blocks)


def attend_body(length_ref, q_ref, k_ref, fresh_ref, out_ref, score_ref):
    request = pl.program_id(0)
    length = length_ref[request]
    steps, heads = q_ref.shape[0], q_ref.shape[3]
    slots = k_ref.shape[2]
    q = jnp.concatenate([q_ref[s, 0].T for s in range(steps)], axis=0)
    fresh = fresh_ref[0]
    fresh_scores = (
        lax.dot_general(q, fresh, (((1,), (1,)), ((), ())), preferred_element_type=jnp.float32)
        * SCORE_SCALE
    )
    row_step = lax.broadcasted_iota(jnp.int32, fresh_scores.shape, 0) // heads
    fresh_lane = lax.broadcasted_iota(jnp.int32, fresh_scores.shape, 1)
    fresh_scores = jnp.where(fresh_lane <= row_step, fresh_scores, -jnp.inf)
    top = jnp.max(fresh_scores, axis=1, keepdims=True)
    for start in range(0, slots, SLOT_CHUNK):
        cols = pl.ds(start, SLOT_CHUNK)
        scores = jnp.dot(q, k_ref[0, :, cols], preferred_element_type=jnp.float32) * SCORE_SCALE
        slot = lax.broadcasted_iota(jnp.int32, scores.shape, 1) + start
        scores = jnp.where(slot < length, scores, -jnp.inf)
        score_ref[:, cols] = scores
        top = jnp.maximum(top, jnp.max(scores, axis=1, keepdims=True))
    fresh_exp = jnp.exp(fresh_scores - top)
    denominator = jnp.sum(fresh_exp, axis=1, keepdims=True)
    total = jnp.dot(
        fresh_exp.astype(jnp.bfloat16), fresh[:, :KV_RANK], preferred_element_type=jnp.float32
    )
    for start in range(0, slots, SLOT_CHUNK):
        cols = pl.ds(start, SLOT_CHUNK)
        weights = jnp.exp(score_ref[:, cols] - top)
        denominator = denominator + jnp.sum(weights, axis=1, keepdims=True)
        total = total + lax.dot_general(
            weights.astype(jnp.bfloat16),
            k_ref[0, :KV_RANK, cols],
            (((1,), (1,)), ((), ())),
            preferred_element_type=jnp.float32,
        )
    result = (total / denominator).astype(jnp.bfloat16)
    for s in range(steps):
        out_ref[s, 0] = result[s * heads : (s + 1) * heads]


def attend(queries, kv_cache, new_keys, cache_lengths):
    steps, requests, heads, width = queries.shape
    slots = kv_cache.shape[1]
    q_t = jnp.swapaxes(queries, 2, 3)
    k_t = jnp.swapaxes(kv_cache, 1, 2)
    fresh = jnp.pad(jnp.swapaxes(new_keys, 0, 1), ((0, 0), (0, 16 - steps), (0, 0)))
    return pl.pallas_call(
        attend_body,
        out_shape=jax.ShapeDtypeStruct((steps, requests, heads, KV_RANK), jnp.bfloat16),
        grid=(requests,),
        in_specs=[
            pl.BlockSpec(memory_space=pltpu.SMEM),
            pl.BlockSpec((steps, 1, width, heads), lambda r: (0, r, 0, 0)),
            pl.BlockSpec((1, width, slots), lambda r: (r, 0, 0)),
            pl.BlockSpec((1, 16, width), lambda r: (r, 0, 0)),
        ],
        out_specs=pl.BlockSpec((steps, 1, heads, KV_RANK), lambda r: (0, r, 0, 0)),
        scratch_shapes=[pltpu.VMEM((steps * heads, slots), jnp.float32)],
        compiler_params=pltpu.CompilerParams(vmem_limit_bytes=ATTEND_VMEM),
        cost_estimate=pl.CostEstimate(
            flops=2 * steps * requests * heads * slots * (width + KV_RANK),
            bytes_accessed=2 * requests * (slots * width + steps * heads * (width + KV_RANK)),
            transcendentals=steps * requests * heads * slots,
        ),
        name="attend",
    )(cache_lengths, in_hbm(q_t), in_hbm(k_t), fresh)


def join_body(*refs):
    in_refs, out_refs = refs[:-SIDE], refs[-SIDE:]
    half = len(in_refs) // 2
    mine, back = (
        jnp.concatenate([r[...].astype(jnp.float32) for r in part], axis=0)
        for part in (in_refs[:half], in_refs[half:])
    )
    total = (mine + back).astype(jnp.bfloat16)
    for out_ref, piece in zip(out_refs, cut(total, SIDE)):
        out_ref[...] = piece


def join(mine, back):
    rows, width = sum(b.shape[0] for b in back), back[0].shape[1]
    piece = jax.ShapeDtypeStruct((rows // SIDE, width), back[0].dtype)
    return pl.pallas_call(
        join_body,
        out_shape=[piece] * SIDE,
        compiler_params=pltpu.CompilerParams(vmem_limit_bytes=JOIN_VMEM),
        name="join",
    )(*mine, *back)


def hold_body(*refs):
    pass


def hold(blocks, after):
    anywhere = pl.BlockSpec(memory_space=pl.ANY)
    return pl.pallas_call(
        hold_body,
        out_shape=[jax.ShapeDtypeStruct(b.shape, b.dtype) for b in blocks],
        in_specs=[anywhere] * (len(blocks) + len(after)),
        out_specs=[anywhere] * len(blocks),
        input_output_aliases={i: i for i in range(len(blocks))},
        compiler_params=pltpu.CompilerParams(vmem_limit_bytes=1024 * 1024),
        name="hold",
    )(*blocks, *after)


def resident_body(*refs, count):
    sems, outs = refs[-1], refs[-1 - count : -1]
    copies = [pltpu.make_async_copy(refs[i], outs[i], sems.at[i]) for i in range(count)]
    for copy in copies:
        copy.start()
    for copy in copies:
        copy.wait()


def resident(weights, after):
    count = len(weights)
    return pl.pallas_call(
        functools.partial(resident_body, count=count),
        out_shape=[pltpu.VMEM(w.shape, w.dtype) for w in weights],
        in_specs=[pl.BlockSpec(memory_space=pltpu.HBM)] * count
        + [pl.BlockSpec(memory_space=pl.ANY)] * len(after),
        out_specs=[pl.BlockSpec(memory_space=pltpu.VMEM)] * count,
        scratch_shapes=[pltpu.SemaphoreType.DMA((count,))],
        compiler_params=pltpu.CompilerParams(vmem_limit_bytes=SMALL_VMEM),
        name="resident",
    )(*[in_hbm(w) for w in weights], *after)


def expert_body(*refs, count):
    token_refs = refs[:count]
    gate_w, up_w, down_w = refs[count : count + 3]
    out_refs = refs[-count:]
    features = gate_w.shape[0]
    heights = [r.shape[0] for r in token_refs]

    def tokens(at):
        return jnp.concatenate([r[:, at] for r in token_refs], axis=0)

    gates = tokens(pl.ds(features, GATE_LANES)).astype(jnp.float32)
    core, y, z = (lax.axis_index(name) for name in ("c", "y", "z"))
    expert = (core * SIDE + y) * 2 + (z >= SIDE // 2).astype(jnp.int32)
    lanes = lax.broadcasted_iota(jnp.int32, gates.shape, 1)
    column = jnp.sum(jnp.where(lanes == expert, gates, 0.0), axis=1, keepdims=True)

    chunks = [pl.ds(i, FEATURE_CHUNK) for i in range(0, features, FEATURE_CHUNK)]
    gate = up = None
    for at in chunks:
        rows = tokens(at)
        more_gate = jnp.dot(rows, gate_w[at, :], preferred_element_type=jnp.float32)
        more_up = jnp.dot(rows, up_w[at, :], preferred_element_type=jnp.float32)
        gate = more_gate if gate is None else gate + more_gate
        up = more_up if up is None else up + more_up
    hidden = (gate / (1.0 + jnp.exp(-gate)) * up).astype(jnp.bfloat16)
    for at in chunks:
        outs = jnp.dot(hidden, down_w[:, at], preferred_element_type=jnp.float32)
        outs = (outs * column).astype(jnp.bfloat16)
        top = 0
        for out_ref, height in zip(out_refs, heights):
            out_ref[:, at] = outs[top : top + height]
            top += height


def expert_call(blocks, weights, after):
    count = len(blocks)
    heights = [b.shape[0] for b in blocks]
    all_rows = sum(heights)
    features, hidden_units = weights[0].shape
    whole = pl.BlockSpec(memory_space=pltpu.VMEM)
    return pl.pallas_call(
        functools.partial(expert_body, count=count),
        out_shape=[jax.ShapeDtypeStruct((h, features), jnp.bfloat16) for h in heights],
        in_specs=[whole] * (count + 3) + [pl.BlockSpec(memory_space=pl.ANY)] * len(after),
        out_specs=[whole] * count,
        compiler_params=pltpu.CompilerParams(vmem_limit_bytes=EXPERT_VMEM),
        cost_estimate=pl.CostEstimate(
            flops=6 * all_rows * features * hidden_units,
            bytes_accessed=4 * all_rows * features,
            transcendentals=all_rows * hidden_units,
        ),
        name="experts",
    )(*blocks, *weights, *after)


def routed_block(
    hidden_state, ffn_gain, expert_ids, expert_gates, w_gate, w_up, w_down, attended
):
    steps, requests, features = hidden_state.shape
    near, middle, far = ("z", "x"), ("y", "z"), ("x", "y")
    own = prepare(hidden_state, ffn_gain, expert_ids, expert_gates)
    own = stack(collect(own, near))
    pieces = collect(own, middle)
    first, second = stack(pieces[:2]), stack(pieces[2:])

    def apply_expert(blocks, after):
        theirs = other_core(stack(blocks))
        *mine, theirs = expert_call([*blocks, theirs], weights, after)
        return mine, other_core(theirs)

    def merge(mine, received):
        return [add_up(pair) for pair in zip(mine, cut(received, len(mine)))]

    def neighbours(block):
        return [shift(block, far, -1), shift(block, far, 1)]

    arrived = neighbours(first) + neighbours(second)
    weights = resident([w_gate, w_up, w_down], [in_hbm(attended), *arrived[:2]])
    own, *arrived = hold([stack([first, second]), *arrived], weights)
    opposite = [shift(arrived[0], far, -1), shift(arrived[3], far, 1)]
    theirs = [other_core(stack(pair)) for pair in (arrived[:2], arrived[2:])]
    outs = expert_call(arrived, weights, [])
    back_first = expert_call(theirs[:1], weights, outs[:1])
    back_second = expert_call(theirs[1:], weights, back_first)
    sums = merge(outs[:2], other_core(back_first[0])) + merge(outs[2:], other_core(back_second[0]))
    home = [shift(stack(sums[0::2]), far, 1), shift(stack(sums[1::2]), far, -1)]
    own_out, own_back = apply_expert([own], back_second)
    opposite = hold(opposite, [*sums, *own_out])
    theirs = [other_core(block) for block in opposite]
    outs = expert_call([*opposite, *theirs], weights, own_out)
    back = [other_core(block) for block in hold(outs[2:], [*home, own_back])]
    own_sum = add_up([own_out[0], own_back])
    far_sum = add_up(send_home(join(outs[:2], back), middle))
    far_sum = shift(far_sum, far, 2)
    blocks = [cut(block, SIDE) for block in (own_sum, *home)]
    summed = send_home([add_up(p) for p in zip(*blocks)], middle)
    summed = add_up([*summed, far_sum])
    summed = add_up(send_home(cut(summed, SIDE), near))
    return summed.reshape(steps, requests, features)


def on_device(
    hidden_state,
    ffn_gain,
    expert_ids,
    expert_gates,
    w_gate,
    w_up,
    w_down,
    queries,
    kv_cache,
    new_keys,
    cache_lengths,
):
    attended = attend(queries, kv_cache, new_keys, cache_lengths)
    routed = routed_block(
        hidden_state, ffn_gain, expert_ids, expert_gates, w_gate, w_up, w_down, attended
    )
    return attended, routed


def solution(mesh):
    chips = Mesh(mesh.devices.reshape(2, SIDE, SIDE, SIDE), AXES)
    placed = (
        P(None, AXES, None),
        P(),
        P(None, AXES, None),
        P(None, AXES, None),
        P(None, AXES),
        P(None, AXES),
        P(AXES, None),
        P(None, AXES, None, None),
        P(AXES, None, None),
        P(None, AXES, None),
        P(AXES),
    )
    return jax.shard_map(
        on_device,
        mesh=chips,
        in_specs=placed,
        out_specs=(P(None, AXES, None, None), P(None, AXES, None)),
        check_vma=False,
    )
```

```python
import functools
import math

import jax
import jax.numpy as jnp
from jax import lax
from jax.experimental import pallas as pl
from jax.experimental.pallas import tpu as pltpu
from jax.sharding import Mesh
from jax.sharding import PartitionSpec as P

KV_RANK = 512
EPS = 1e-06
SCORE_SCALE = 1.0 / math.sqrt(192.0)
AXES = ("c", "y", "z", "x")
SIDE = 4
GATE_LANES = 128
SLOT_CHUNK = 512
FEATURE_CHUNK = 3584
SMALL_VMEM = 4 * 1024 * 1024
ATTEND_VMEM = 16 * 1024 * 1024
JOIN_VMEM = 12 * 1024 * 1024
EXPERT_VMEM = 12 * 1024 * 1024


def device_number(c, y, z, x):
    return ((c * SIDE + y) * SIDE + z) * SIDE + x


def shifted_pairs(axis_of_core, distance):
    pairs = []
    for c in range(2):
        for y in range(SIDE):
            for z in range(SIDE):
                for x in range(SIDE):
                    place = {"y": y, "z": z, "x": x}
                    axis = axis_of_core[c]
                    place[axis] = (place[axis] + distance) % SIDE
                    pairs.append((device_number(c, y, z, x), device_number(c, **place)))
    return pairs


def shift(block, axis_of_core, distance):
    return lax.ppermute(block, AXES, shifted_pairs(axis_of_core, distance))


def other_core(block):
    return lax.ppermute(block, "c", [(0, 1), (1, 0)])


def collect(block, axis_of_core):
    return [
        block,
        shift(block, axis_of_core, -1),
        shift(block, axis_of_core, 1),
        shift(block, axis_of_core, 2),
    ]


def send_home(blocks, axis_of_core):
    return [
        blocks[0],
        shift(blocks[1], axis_of_core, 1),
        shift(blocks[2], axis_of_core, -1),
        shift(blocks[3], axis_of_core, 2),
    ]


def add_up(blocks):
    total = blocks[0].astype(jnp.float32)
    for block in blocks[1:]:
        total = total + block.astype(jnp.float32)
    return total.astype(jnp.bfloat16)


def cut(rows, parts):
    size = rows.shape[0] // parts
    return [rows[i * size : (i + 1) * size] for i in range(parts)]


def prepare_body(state_in, gain_in, id_in, gate_in, out_ref, state_ref, gain_ref, id_ref, gate_ref, sems):
    pairs = ((state_in, state_ref), (gain_in, gain_ref), (id_in, id_ref), (gate_in, gate_ref))
    copies = [pltpu.make_async_copy(a, b, sems.at[i]) for i, (a, b) in enumerate(pairs)]
    for copy in copies:
        copy.start()
    for copy in copies:
        copy.wait()
    steps, requests, features = state_ref.shape
    gain = gain_ref[...].astype(jnp.float32)
    lanes = lax.broadcasted_iota(jnp.int32, (requests, GATE_LANES), 1)
    for s in range(steps):
        rows = pl.ds(s * requests, requests)
        values = state_ref[s].astype(jnp.float32)
        factor = lax.rsqrt(jnp.mean(values * values, axis=-1, keepdims=True) + EPS)
        for j in range(gain.shape[0]):
            at = slice(j * GATE_LANES, (j + 1) * GATE_LANES)
            scaled = values[:, at] * factor * gain[j : j + 1]
            out_ref[rows, at] = scaled.astype(jnp.bfloat16)
        ids, gates = id_ref[s], gate_ref[s].astype(jnp.float32)
        table = jnp.zeros((requests, GATE_LANES), jnp.float32)
        for k in range(ids.shape[1]):
            table = table + jnp.where(lanes == ids[:, k : k + 1], gates[:, k : k + 1], 0.0)
        out_ref[rows, features:] = table.astype(jnp.bfloat16)


def prepare(hidden_state, ffn_gain, expert_ids, expert_gates):
    steps, requests, features = hidden_state.shape
    inputs = (hidden_state, ffn_gain.reshape(-1, GATE_LANES), expert_ids, expert_gates)
    inputs = [in_hbm(a) for a in inputs]
    return pl.pallas_call(
        prepare_body,
        out_shape=jax.ShapeDtypeStruct((steps * requests, features + GATE_LANES), jnp.bfloat16),
        in_specs=[pl.BlockSpec(memory_space=pltpu.HBM)] * len(inputs),
        scratch_shapes=[pltpu.VMEM(a.shape, a.dtype) for a in inputs]
        + [pltpu.SemaphoreType.DMA((len(inputs),))],
        compiler_params=pltpu.CompilerParams(vmem_limit_bytes=SMALL_VMEM),
        name="prepare",
    )(*inputs)


def in_hbm(array):
    return pltpu.with_memory_space_constraint(array, pltpu.HBM)


def stack_body(*refs):
    rows = refs[0].shape[0]
    for i, ref in enumerate(refs[:-1]):
        refs[-1][pl.ds(i * rows, rows), :] = ref[...]


def stack(blocks):
    if len(blocks) == 1:
        return blocks[0]
    rows, width = blocks[0].shape
    return pl.pallas_call(
        stack_body,
        out_shape=jax.ShapeDtypeStruct((rows * len(blocks), width), blocks[0].dtype),
        compiler_params=pltpu.CompilerParams(vmem_limit_bytes=SMALL_VMEM),
        name="stack",
    )(*blocks)


def attend_body(length_ref, q_ref, k_ref, fresh_ref, out_ref, score_ref):
    request = pl.program_id(0)
    length = length_ref[request]
    steps, heads = q_ref.shape[0], q_ref.shape[3]
    slots = k_ref.shape[2]
    q = jnp.concatenate([q_ref[s, 0].T for s in range(steps)], axis=0)
    fresh = fresh_ref[0]
    fresh_scores = (
        lax.dot_general(q, fresh, (((1,), (1,)), ((), ())), preferred_element_type=jnp.float32)
        * SCORE_SCALE
    )
    row_step = lax.broadcasted_iota(jnp.int32, fresh_scores.shape, 0) // heads
    fresh_lane = lax.broadcasted_iota(jnp.int32, fresh_scores.shape, 1)
    fresh_scores = jnp.where(fresh_lane <= row_step, fresh_scores, -jnp.inf)
    top = jnp.max(fresh_scores, axis=1, keepdims=True)
    for start in range(0, slots, SLOT_CHUNK):
        cols = pl.ds(start, SLOT_CHUNK)
        scores = jnp.dot(q, k_ref[0, :, cols], preferred_element_type=jnp.float32) * SCORE_SCALE
        slot = lax.broadcasted_iota(jnp.int32, scores.shape, 1) + start
        scores = jnp.where(slot < length, scores, -jnp.inf)
        score_ref[:, cols] = scores
        top = jnp.maximum(top, jnp.max(scores, axis=1, keepdims=True))
    fresh_exp = jnp.exp(fresh_scores - top)
    denominator = jnp.sum(fresh_exp, axis=1, keepdims=True)
    total = jnp.dot(
        fresh_exp.astype(jnp.bfloat16), fresh[:, :KV_RANK], preferred_element_type=jnp.float32
    )
    for start in range(0, slots, SLOT_CHUNK):
        cols = pl.ds(start, SLOT_CHUNK)
        weights = jnp.exp(score_ref[:, cols] - top)
        denominator = denominator + jnp.sum(weights, axis=1, keepdims=True)
        total = total + lax.dot_general(
            weights.astype(jnp.bfloat16),
            k_ref[0, :KV_RANK, cols],
            (((1,), (1,)), ((), ())),
            preferred_element_type=jnp.float32,
        )
    result = (total / denominator).astype(jnp.bfloat16)
    for s in range(steps):
        out_ref[s, 0] = result[s * heads : (s + 1) * heads]


def attend(queries, kv_cache, new_keys, cache_lengths):
    steps, requests, heads, width = queries.shape
    slots = kv_cache.shape[1]
    q_t = jnp.swapaxes(queries, 2, 3)
    k_t = jnp.swapaxes(kv_cache, 1, 2)
    fresh = jnp.pad(jnp.swapaxes(new_keys, 0, 1), ((0, 0), (0, 16 - steps), (0, 0)))
    return pl.pallas_call(
        attend_body,
        out_shape=jax.ShapeDtypeStruct((steps, requests, heads, KV_RANK), jnp.bfloat16),
        grid=(requests,),
        in_specs=[
            pl.BlockSpec(memory_space=pltpu.SMEM),
            pl.BlockSpec((steps, 1, width, heads), lambda r: (0, r, 0, 0)),
            pl.BlockSpec((1, width, slots), lambda r: (r, 0, 0)),
            pl.BlockSpec((1, 16, width), lambda r: (r, 0, 0)),
        ],
        out_specs=pl.BlockSpec((steps, 1, heads, KV_RANK), lambda r: (0, r, 0, 0)),
        scratch_shapes=[pltpu.VMEM((steps * heads, slots), jnp.float32)],
        compiler_params=pltpu.CompilerParams(vmem_limit_bytes=ATTEND_VMEM),
        cost_estimate=pl.CostEstimate(
            flops=2 * steps * requests * heads * slots * (width + KV_RANK),
            bytes_accessed=2 * requests * (slots * width + steps * heads * (width + KV_RANK)),
            transcendentals=steps * requests * heads * slots,
        ),
        name="attend",
    )(cache_lengths, in_hbm(q_t), in_hbm(k_t), fresh)


def join_body(*refs):
    in_refs, out_refs = refs[:-SIDE], refs[-SIDE:]
    half = len(in_refs) // 2
    mine, back = (
        jnp.concatenate([r[...].astype(jnp.float32) for r in part], axis=0)
        for part in (in_refs[:half], in_refs[half:])
    )
    total = (mine + back).astype(jnp.bfloat16)
    for out_ref, piece in zip(out_refs, cut(total, SIDE)):
        out_ref[...] = piece


def join(mine, back):
    rows, width = sum(b.shape[0] for b in back), back[0].shape[1]
    piece = jax.ShapeDtypeStruct((rows // SIDE, width), back[0].dtype)
    return pl.pallas_call(
        join_body,
        out_shape=[piece] * SIDE,
        compiler_params=pltpu.CompilerParams(vmem_limit_bytes=JOIN_VMEM),
        name="join",
    )(*mine, *back)


def hold_body(*refs):
    pass


def hold(blocks, after):
    anywhere = pl.BlockSpec(memory_space=pl.ANY)
    return pl.pallas_call(
        hold_body,
        out_shape=[jax.ShapeDtypeStruct(b.shape, b.dtype) for b in blocks],
        in_specs=[anywhere] * (len(blocks) + len(after)),
        out_specs=[anywhere] * len(blocks),
        input_output_aliases={i: i for i in range(len(blocks))},
        compiler_params=pltpu.CompilerParams(vmem_limit_bytes=1024 * 1024),
        name="hold",
    )(*blocks, *after)


def resident_body(*refs, count):
    sems, outs = refs[-1], refs[-1 - count : -1]
    copies = [pltpu.make_async_copy(refs[i], outs[i], sems.at[i]) for i in range(count)]
    for copy in copies:
        copy.start()
    for copy in copies:
        copy.wait()


def resident(weights, after):
    count = len(weights)
    return pl.pallas_call(
        functools.partial(resident_body, count=count),
        out_shape=[pltpu.VMEM(w.shape, w.dtype) for w in weights],
        in_specs=[pl.BlockSpec(memory_space=pltpu.HBM)] * count
        + [pl.BlockSpec(memory_space=pl.ANY)] * len(after),
        out_specs=[pl.BlockSpec(memory_space=pltpu.VMEM)] * count,
        scratch_shapes=[pltpu.SemaphoreType.DMA((count,))],
        compiler_params=pltpu.CompilerParams(vmem_limit_bytes=SMALL_VMEM),
        name="resident",
    )(*[in_hbm(w) for w in weights], *after)


def expert_body(*refs, count):
    token_refs = refs[:count]
    gate_w, up_w, down_w = refs[count : count + 3]
    out_refs = refs[-count:]
    features = gate_w.shape[0]
    heights = [r.shape[0] for r in token_refs]

    def tokens(at):
        return jnp.concatenate([r[:, at] for r in token_refs], axis=0)

    gates = tokens(pl.ds(features, GATE_LANES)).astype(jnp.float32)
    core, y, z = (lax.axis_index(name) for name in ("c", "y", "z"))
    expert = (core * SIDE + y) * 2 + (z >= SIDE // 2).astype(jnp.int32)
    lanes = lax.broadcasted_iota(jnp.int32, gates.shape, 1)
    column = jnp.sum(jnp.where(lanes == expert, gates, 0.0), axis=1, keepdims=True)

    chunks = [pl.ds(i, FEATURE_CHUNK) for i in range(0, features, FEATURE_CHUNK)]
    gate = up = None
    for at in chunks:
        rows = tokens(at)
        more_gate = jnp.dot(rows, gate_w[at, :], preferred_element_type=jnp.float32)
        more_up = jnp.dot(rows, up_w[at, :], preferred_element_type=jnp.float32)
        gate = more_gate if gate is None else gate + more_gate
        up = more_up if up is None else up + more_up
    hidden = (gate / (1.0 + jnp.exp(-gate)) * up).astype(jnp.bfloat16)
    for at in chunks:
        outs = jnp.dot(hidden, down_w[:, at], preferred_element_type=jnp.float32)
        outs = (outs * column).astype(jnp.bfloat16)
        top = 0
        for out_ref, height in zip(out_refs, heights):
            out_ref[:, at] = outs[top : top + height]
            top += height


def expert_call(blocks, weights, after):
    count = len(blocks)
    heights = [b.shape[0] for b in blocks]
    all_rows = sum(heights)
    features, hidden_units = weights[0].shape
    whole = pl.BlockSpec(memory_space=pltpu.VMEM)
    return pl.pallas_call(
        functools.partial(expert_body, count=count),
        out_shape=[jax.ShapeDtypeStruct((h, features), jnp.bfloat16) for h in heights],
        in_specs=[whole] * (count + 3) + [pl.BlockSpec(memory_space=pl.ANY)] * len(after),
        out_specs=[whole] * count,
        compiler_params=pltpu.CompilerParams(vmem_limit_bytes=EXPERT_VMEM),
        cost_estimate=pl.CostEstimate(
            flops=6 * all_rows * features * hidden_units,
            bytes_accessed=4 * all_rows * features,
            transcendentals=all_rows * hidden_units,
        ),
        name="experts",
    )(*blocks, *weights, *after)


def routed_block(
    hidden_state, ffn_gain, expert_ids, expert_gates, w_gate, w_up, w_down, attended
):
    steps, requests, features = hidden_state.shape
    near, middle, far = ("z", "x"), ("y", "z"), ("x", "y")
    own = prepare(hidden_state, ffn_gain, expert_ids, expert_gates)
    own = stack(collect(own, near))
    pieces = collect(own, middle)
    first, second = stack(pieces[:2]), stack(pieces[2:])

    def apply_expert(blocks, after):
        theirs = other_core(stack(blocks))
        *mine, theirs = expert_call([*blocks, theirs], weights, after)
        return mine, other_core(theirs)

    def merge(mine, received):
        return [add_up(pair) for pair in zip(mine, cut(received, len(mine)))]

    def neighbours(block):
        return [shift(block, far, -1), shift(block, far, 1)]

    arrived = neighbours(first) + neighbours(second)
    weights = resident([w_gate, w_up, w_down], [in_hbm(attended), *arrived[:2]])
    own, *arrived = hold([stack([first, second]), *arrived], weights)
    opposite = [shift(arrived[0], far, -1), shift(arrived[3], far, 1)]
    theirs = [other_core(stack(pair)) for pair in (arrived[:2], arrived[2:])]
    outs = expert_call(arrived, weights, [])
    back_first = expert_call(theirs[:1], weights, outs[:1])
    back_second = expert_call(theirs[1:], weights, back_first)
    sums = merge(outs[:2], other_core(back_first[0])) + merge(outs[2:], other_core(back_second[0]))
    home = [shift(stack(sums[0::2]), far, 1), shift(stack(sums[1::2]), far, -1)]
    own_out, own_back = apply_expert([own], back_second)
    opposite = hold(opposite, [*sums, *own_out])
    theirs = [other_core(block) for block in opposite]
    outs = expert_call([*opposite, *theirs], weights, own_out)
    back = [other_core(block) for block in hold(outs[2:], [*home, own_back])]
    own_sum = add_up([own_out[0], own_back])
    far_sum = add_up(send_home(join(outs[:2], back), middle))
    far_sum = shift(far_sum, far, 2)
    blocks = [cut(block, SIDE) for block in (own_sum, *home)]
    summed = send_home([add_up(p) for p in zip(*blocks)], middle)
    summed = add_up([*summed, far_sum])
    summed = add_up(send_home(cut(summed, SIDE), near))
    return summed.reshape(steps, requests, features)


def on_device(
    hidden_state,
    ffn_gain,
    expert_ids,
    expert_gates,
    w_gate,
    w_up,
    w_down,
    queries,
    kv_cache,
    new_keys,
    cache_lengths,
):
    attended = attend(queries, kv_cache, new_keys, cache_lengths)
    routed = routed_block(
        hidden_state, ffn_gain, expert_ids, expert_gates, w_gate, w_up, w_down, attended
    )
    return attended, routed


def solution(mesh):
    chips = Mesh(mesh.devices.reshape(2, SIDE, SIDE, SIDE), AXES)
    placed = (
        P(None, AXES, None),
        P(),
        P(None, AXES, None),
        P(None, AXES, None),
        P(None, AXES),
        P(None, AXES),
        P(AXES, None),
        P(None, AXES, None, None),
        P(AXES, None, None),
        P(None, AXES, None),
        P(AXES),
    )
    return jax.shard_map(
        on_device,
        mesh=chips,
        in_specs=placed,
        out_specs=(P(None, AXES, None, None), P(None, AXES, None)),
        check_vma=False,
    )
```
